32 devices in a mesh: term: 2 (over x), sector: 16 (over z, y, core).
Axes of the slice: x: 2, y: 2, z: 4, core: 2. Of those that a mesh axis runs over, the one named last changes fastest.
Arguments:
- wave_tiles: bfloat16 [256, 2, 128, 128], P('sector'), may hold values from -6 to 6
- left_env: bfloat16 [2, 16, 128, 128], P('term', 'sector'), may hold values from -0.5 to 0.5
- right_env: bfloat16 [2, 16, 128, 128], P('term', 'sector'), may hold values from -0.5 to 0.5
- send_list: int32 [16, 32], P('sector'), may hold values from -1 to 15, as said below
- left_tasks: int32 [2, 16, 96, 3], P('term', 'sector'), may hold values from 0 to 31, as said below
- right_tasks: int32 [2, 16, 256, 3], P('term', 'sector'), may hold values from 0 to 31, as said below
Outputs:
- sigma: float32 [256, 2, 128, 128], P('sector', None, 'term')
The draws below stay inside these ranges and needn't reach their ends.
Inputs may be any that keep to these rules, and one draw needn't show every extreme that they name: send_list[s, o * 2 + c] is a tile index local to sender s, or -1 for an empty slot; some owner drawn from the seed receives a full 2 tiles from every sender. `left_tasks`: entries 0, 1, 2 lie below 16, 32 and 32. `right_tasks`: entries 0, 1, 2 lie below 32, 16 and 16.
All inputs are finite; a program needn't handle non-finite values.
Results may differ from the reference program's by a relative error of at most 0.0029.
Values may be sent and summed in bfloat16 or wider, within the bound.
No kernel may reach another device: no remote copies, remote signals or barrier semaphores. Data moves between devices by JAX's collectives and lax.ppermute only.
A program may use at most 128 MiB of HBM per device.

```python
import jax
import jax.numpy as jnp
from jax import lax

TILE_DIM = 128
VECTORS = 2
CAPACITY = 2
TILE_DEV = 16
LEFT_TASKS = 96
RIGHT_TASKS = 256
INTER_TILES = 32
OWNERS = 16
GROUPS = 2
SEND_SLOTS = 32
ENV_TILES = 16
ALL_TILES = 256


def draw_send_list(key, part):
    key_weight, key_live, key_full, key_index = jax.random.split(key, 4)
    weights = jax.random.randint(key_weight, (OWNERS,), 3, 8)
    rolls = jax.random.randint(key_live, (OWNERS, OWNERS, CAPACITY), 0, 8)
    live = rolls < weights[None, :, None]
    full_owner = jax.random.randint(key_full, (), 0, OWNERS)
    live = live | (jnp.arange(OWNERS) == full_owner)[None, :, None]
    index = jax.random.randint(key_index, (OWNERS, OWNERS, CAPACITY), 0, TILE_DEV)
    return jnp.where(live, index, -1).reshape(OWNERS, SEND_SLOTS).astype(jnp.int32)


def draw_left_tasks(key, part):
    key_env, key_slot, key_inter = jax.random.split(key, 3)
    shape = (GROUPS, OWNERS, LEFT_TASKS)
    columns = [jax.random.randint(key_env, shape, 0, ENV_TILES), jax.random.randint(key_slot, shape, 0, SEND_SLOTS), jax.random.randint(key_inter, shape, 0, INTER_TILES)]
    return jnp.stack(columns, axis=-1).astype(jnp.int32)


def draw_right_tasks(key, part):
    key_inter, key_env, key_out = jax.random.split(key, 3)
    shape = (GROUPS, OWNERS, RIGHT_TASKS)
    columns = [jax.random.randint(key_inter, shape, 0, INTER_TILES), jax.random.randint(key_env, shape, 0, ENV_TILES), jax.random.randint(key_out, shape, 0, TILE_DEV)]
    return jnp.stack(columns, axis=-1).astype(jnp.int32)


def shard_levels(rng, dims, cuts, least, largest):
    loudness, own = 1.0, jax.random.fold_in(rng, 6)
    for position, shards_of in cuts:
        steps = jnp.exp(jax.random.uniform(jax.random.fold_in(own, position), (shards_of,), jnp.float32, least / len(cuts), largest / len(cuts)))
        loudness = loudness * jnp.repeat(steps, dims[position] // shards_of).reshape([-1 if axis == position else 1 for axis in range(len(dims))])
    return loudness


def gaussian(rng, extent, spread, reach, cuts=(), kind=jnp.bfloat16):
    drawn = jax.random.normal(rng, extent, jnp.float32) * spread
    if len(cuts) > 0:
        drawn = shard_levels(rng, extent, cuts, -0.22, 0.18) * drawn
    return jnp.clip(drawn, min=-reach, max=reach).astype(kind)


def setup_inputs(seed: int = 0) -> dict:
    splits = jax.random.split(jax.random.key(seed), 7)
    wave_tiles = gaussian(splits[0], (ALL_TILES, VECTORS, TILE_DIM, TILE_DIM), 1.0, 6.0, ((0, 16),))
    left_env = gaussian(splits[1], (GROUPS, ENV_TILES, TILE_DIM, TILE_DIM), TILE_DIM ** -0.5, 0.5, ((0, 2), (1, 16)))
    right_env = gaussian(splits[2], (GROUPS, ENV_TILES, TILE_DIM, TILE_DIM), TILE_DIM ** -0.5, 0.5, ((0, 2), (1, 16)))
    send_list = draw_send_list(jax.random.fold_in(splits[6], 71), 0)
    left_tasks = draw_left_tasks(jax.random.fold_in(splits[6], 71), 0)
    right_tasks = draw_right_tasks(jax.random.fold_in(splits[6], 71), 0)
    return {"wave_tiles": wave_tiles, "left_env": left_env, "right_env": right_env, "send_list": send_list, "left_tasks": left_tasks, "right_tasks": right_tasks}


def one_group(received, env_left, env_right, left_rows, right_rows):
    left_tiles = jnp.take(env_left, left_rows[:, 0], axis=0).astype(jnp.float32)
    wave_part = jnp.take(received, left_rows[:, 1], axis=0).astype(jnp.float32)
    products = jnp.einsum("bij,bvjk->bvik", left_tiles, wave_part, precision=lax.Precision.HIGHEST)
    inter = jax.ops.segment_sum(products, left_rows[:, 2], num_segments=INTER_TILES).astype(jnp.bfloat16)
    inter_part = jnp.take(inter, right_rows[:, 0], axis=0).astype(jnp.float32)
    right_tiles = jnp.take(env_right, right_rows[:, 1], axis=0).astype(jnp.float32)
    products = jnp.einsum("bvij,bjk->bvik", inter_part, right_tiles, precision=lax.Precision.HIGHEST)
    return jax.ops.segment_sum(products, right_rows[:, 2], num_segments=TILE_DEV)


def reference(wave_tiles, left_env, right_env, send_list, left_tasks, right_tasks):
    by_owner = jnp.transpose(send_list.reshape(OWNERS, OWNERS, CAPACITY), (1, 0, 2))
    left_owner = jnp.swapaxes(left_tasks, 0, 1)
    right_owner = jnp.swapaxes(right_tasks, 0, 1)
    senders = jnp.arange(OWNERS, dtype=jnp.int32)

    def per_owner(inputs):
        local_list, left_rows, right_rows = inputs
        global_index = (senders[:, None] * TILE_DEV + jnp.maximum(local_list, 0)).reshape(-1).astype(jnp.int32)
        live = (local_list >= 0).reshape(-1)
        received = jnp.where(live[:, None, None, None], jnp.take(wave_tiles, global_index, axis=0), jnp.zeros((), jnp.bfloat16))

        def add_group(total, group_inputs):
            env_left, env_right, left_one, right_one = group_inputs
            return total + one_group(received, env_left, env_right, left_one, right_one), None

        start = jnp.zeros((TILE_DEV, VECTORS, TILE_DIM, TILE_DIM), jnp.float32)
        total, unused = lax.scan(add_group, start, (left_env, right_env, left_rows, right_rows))
        return total

    result = lax.map(per_owner, (by_owner, left_owner, right_owner))
    return result.reshape(ALL_TILES, VECTORS, TILE_DIM, TILE_DIM)
```

```python
import functools

import jax
import jax.numpy as jnp
from jax import lax
from jax.experimental import pallas as pl
from jax.experimental.pallas import tpu as pltpu
from jax.sharding import PartitionSpec as P

INTER_TILES = 32
DEPTH = 8
LEFT_UNROLL = 8
RIGHT_UNROLL = 4


def round_up(value, step):
    return -(-value // step) * step


def butterfly_steps(sectors, terms):
    bits = [bit for bit in range(sectors.bit_length() - 1)]
    order = [("sector", bit) for bit in bits if bit >= 2]
    order += [("sector", bit) for bit in bits if bit == 1]
    order += [("term", bit) for bit in range(terms.bit_length() - 1)]
    order += [("sector", bit) for bit in bits if bit == 0]
    return order


def swap(value, axis, bit):
    size = lax.axis_size(axis)
    return lax.ppermute(value, axis, [(i, i ^ (1 << bit)) for i in range(size)])


def env_place(group, tile, steps):
    group = group ^ lax.axis_index("term")
    tile = tile ^ lax.axis_index("sector")
    place = jnp.zeros_like(tile)
    for turn, (axis, bit) in enumerate(steps):
        source = tile if axis == "sector" else group
        place = place + (((source >> bit) & 1) << turn)
    return place


def schedule(first, second, target, targets, depth, slots, idle):
    count = target.shape[0]
    index = jnp.arange(count, dtype=jnp.int32)
    same = target[:, None] == target[None, :]
    rank = jnp.sum(same & (index[None, :] < index[:, None]), axis=1, dtype=jnp.int32)
    names = jnp.arange(targets, dtype=jnp.int32)
    counts = jnp.sum(target[None, :] == names[:, None], axis=1, dtype=jnp.int32)
    padded = (counts + depth - 1) // depth * depth
    starts = jnp.sum(
        jnp.where(names[None, :] < target[:, None], padded[None, :], 0), axis=1, dtype=jnp.int32
    )
    place = starts + rank
    chosen = place[None, :] == jnp.arange(slots, dtype=jnp.int32)[:, None]

    def pick(values, rest):
        return rest + jnp.sum(jnp.where(chosen, values[None, :] - rest, 0), axis=1, dtype=jnp.int32)

    return jnp.concatenate([pick(first, idle), pick(second, 0), pick(target, 0)])


def products_kernel(
    left_count, slots, share, left, right, side, wave, env_left, env_right, keep, send, acc, inter, total
):
    inters = acc.shape[0]
    rows = acc.shape[1]
    acc[...] = jnp.zeros_like(acc)
    total[...] = jnp.zeros_like(total)

    @pl.loop(0, left_count // LEFT_UNROLL)
    def _(turn):
        done = []
        for step in range(LEFT_UNROLL):
            at = turn * LEFT_UNROLL + step
            product = jnp.dot(
                env_left[left[at]], wave[left[left_count + at]], preferred_element_type=jnp.float32
            )
            done.append((left[2 * left_count + at], product))
        for place, product in done:
            acc[place] += product

    @pl.loop(0, inters // 4)
    def _(turn):
        for step in range(4):
            inter[turn * 4 + step] = acc[turn * 4 + step].astype(jnp.bfloat16)

    inter[inters] = jnp.zeros((rows, inter.shape[2]), jnp.bfloat16)

    @pl.loop(0, slots // (DEPTH * RIGHT_UNROLL))
    def _(turn):
        done = []
        for step in range(RIGHT_UNROLL):
            base = (turn * RIGHT_UNROLL + step) * DEPTH
            first = [inter[right[base + i]] for i in range(DEPTH)]
            second = [env_right[right[slots + base + i]] for i in range(DEPTH)]
            product = jnp.dot(
                jnp.concatenate(first, axis=1),
                jnp.concatenate(second, axis=0),
                preferred_element_type=jnp.float32,
            )
            done.append((right[2 * slots + base], product))
        for place, product in done:
            total[place] += product

    parts = rows // share
    mine = side[0]
    keep[...] = total[:, pl.ds(pl.multiple_of(mine * share, share), share), :]
    for hop in range(1, parts):
        other = lax.rem(mine + hop, parts)
        send[hop - 1] = total[:, pl.ds(pl.multiple_of(other * share, share), share), :].astype(
            jnp.bfloat16
        )


def shards(wave_tiles, left_env, right_env, send_list, left_tasks, right_tasks):
    sectors, terms = lax.axis_size("sector"), lax.axis_size("term")
    tiles, vectors, dim, _ = wave_tiles.shape
    term = lax.axis_index("term")
    blocks = terms // vectors
    rows, share = dim // blocks, dim // terms
    vector, block = term % vectors, term // vectors

    slot_list = send_list[0]
    live = slot_list >= 0
    picked = jnp.take(
        wave_tiles.reshape(tiles * vectors, dim, dim),
        jnp.maximum(slot_list, 0) * vectors + vector,
        axis=0,
    )
    outgoing = jnp.where(live[:, None, None], picked, jnp.zeros((), jnp.bfloat16))
    received = lax.all_to_all(outgoing, "sector", split_axis=0, concat_axis=0, tiled=True)

    steps = butterfly_steps(sectors, terms)
    env = jnp.stack([left_env[0, 0], right_env[0, 0]])[:, None]
    for axis, bit in steps:
        env = jnp.concatenate([env, swap(env, axis, bit)], axis=1)
    env_left, env_right = env[0], env[1]
    env_left = lax.dynamic_slice_in_dim(env_left, block * rows, rows, 1)

    tasks = jnp.concatenate([left_tasks[0, 0], right_tasks[0, 0]], axis=0)
    tasks = lax.all_gather(tasks, "term", axis=0)
    left_rows, right_rows = tasks[:, : left_tasks.shape[2]], tasks[:, left_tasks.shape[2] :]
    groups = jnp.arange(terms, dtype=jnp.int32)[:, None]
    left_count = left_rows.shape[0] * left_rows.shape[1]
    right_count = right_rows.shape[0] * right_rows.shape[1]
    left = jnp.concatenate(
        [
            env_place(groups, left_rows[:, :, 0], steps).reshape(-1),
            left_rows[:, :, 1].reshape(-1),
            (groups * INTER_TILES + left_rows[:, :, 2]).reshape(-1),
        ]
    )
    slots = round_up(right_count + tiles * (DEPTH - 1), DEPTH * RIGHT_UNROLL)
    right = schedule(
        (groups * INTER_TILES + right_rows[:, :, 0]).reshape(-1),
        env_place(groups, right_rows[:, :, 1], steps).reshape(-1),
        right_rows[:, :, 2].reshape(-1),
        tiles,
        DEPTH,
        slots,
        terms * INTER_TILES,
    )
    vmem = pl.BlockSpec(memory_space=pltpu.VMEM)
    smem = pl.BlockSpec(memory_space=pltpu.SMEM)
    inters = terms * INTER_TILES
    keep, send = pl.pallas_call(
        functools.partial(products_kernel, left_count, slots, share),
        out_shape=(
            jax.ShapeDtypeStruct((tiles, share, dim), jnp.float32),
            jax.ShapeDtypeStruct((vectors - 1, tiles, share, dim), jnp.bfloat16),
        ),
        in_specs=[smem, smem, smem, vmem, vmem, vmem],
        out_specs=(vmem, vmem),
        scratch_shapes=[
            pltpu.VMEM((inters, rows, dim), jnp.float32),
            pltpu.VMEM((inters + 1, rows, dim), jnp.bfloat16),
            pltpu.VMEM((tiles, rows, dim), jnp.float32),
        ],
        compiler_params=pltpu.CompilerParams(vmem_limit_bytes=48 << 20),
        name="products",
    )(left, right, vector[None].astype(jnp.int32), received, env_left, env_right)

    pieces = [keep]
    for hop in range(1, vectors):
        pairs = [
            (i, i // vectors * vectors + (i % vectors + hop) % vectors) for i in range(terms)
        ]
        pieces.append(lax.ppermute(send[hop - 1], "term", pairs).astype(jnp.float32))
    result = []
    for place in range(vectors):
        hop = (vector - place) % vectors
        chosen = pieces[0]
        for other in range(1, vectors):
            chosen = jnp.where(hop == other, pieces[other], chosen)
        result.append(chosen)
    return jnp.stack(result, axis=1)


def solution(mesh):
    in_specs = (
        P("sector", None, None, None),
        P("term", "sector", None, None),
        P("term", "sector", None, None),
        P("sector", None),
        P("term", "sector", None, None),
        P("term", "sector", None, None),
    )
    out_specs = P("sector", None, "term", None)
    return jax.shard_map(shards, mesh=mesh, in_specs=in_specs, out_specs=out_specs, check_vma=False)
```

```python
import functools

import jax
import jax.numpy as jnp
from jax import lax
from jax.experimental import pallas as pl
from jax.experimental.pallas import tpu as pltpu
from jax.sharding import PartitionSpec as P

INTER_TILES = 32
DEPTH = 8
PACK_UNROLL = 8
LEFT_UNROLL = 16
RIGHT_UNROLL = 8


def round_up(value, step):
    return -(-value // step) * step


def swap(value, axis, mask):
    size = lax.axis_size(axis)
    return lax.ppermute(value, axis, [(i, i ^ mask) for i in range(size)])


def env_place(group, tile, side):
    sectors, terms = lax.axis_size("sector"), lax.axis_size("term")
    group = group ^ lax.axis_index("term")
    tile = tile ^ lax.axis_index("sector")
    far = sectors // 4
    place = (tile >> 2) + far * (((tile >> 1) & 1) + 2 * group)
    return place + far * 2 * terms * (side + 2 * (tile & 1))


def gather_env(env):
    sectors, terms = lax.axis_size("sector"), lax.axis_size("term")
    far = [env] + [swap(env, "sector", mask << 2) for mask in range(1, sectors // 4)]
    column = jnp.stack(far, axis=1)
    across, over = swap(column, "sector", 2), swap(column, "term", 1)
    corner = jnp.stack([swap(over[0], "sector", 2), swap(across[1], "term", 1)])
    plane = jnp.concatenate([column, across, over, corner], axis=1)
    bit = 2
    while bit < terms:
        plane = jnp.concatenate([plane, swap(plane, "term", bit)], axis=1)
        bit *= 2
    both = jnp.stack([plane, swap(plane, "sector", 1)])
    return both.reshape((-1,) + env.shape[1:])


def pack_kernel(vectors, picks, wave, left, right, out, env, held, sems):
    vector = lax.rem(lax.axis_index("term"), vectors)
    copies = [
        pltpu.make_async_copy(wave.at[:, vector], held, sems.at[0]),
        pltpu.make_async_copy(left.at[0, 0], env.at[0], sems.at[1]),
        pltpu.make_async_copy(right.at[0, 0], env.at[1], sems.at[2]),
    ]
    for copy in copies:
        copy.start()
    for copy in copies:
        copy.wait()

    @pl.loop(0, out.shape[0] // PACK_UNROLL)
    def _(turn):
        for step in range(PACK_UNROLL):
            slot = turn * PACK_UNROLL + step
            tile = picks[0, slot]
            picked = held[jnp.maximum(tile, 0)]
            out[slot] = jnp.where(tile >= 0, picked, jnp.zeros_like(picked))


def schedule(first, second, target, targets, depth, slots, idle):
    count = target.shape[0]
    index = jnp.arange(count, dtype=jnp.int32)
    same = target[:, None] == target[None, :]
    rank = jnp.sum(same & (index[None, :] < index[:, None]), axis=1, dtype=jnp.int32)
    names = jnp.arange(targets, dtype=jnp.int32)
    counts = jnp.sum(target[None, :] == names[:, None], axis=1, dtype=jnp.int32)
    padded = (counts + depth - 1) // depth * depth
    starts = jnp.sum(
        jnp.where(names[None, :] < target[:, None], padded[None, :], 0), axis=1, dtype=jnp.int32
    )
    place = starts + rank
    chosen = place[None, :] == jnp.arange(slots, dtype=jnp.int32)[:, None]

    def pick(values, rest):
        return rest + jnp.sum(jnp.where(chosen, values[None, :] - rest, 0), axis=1, dtype=jnp.int32)

    return jnp.concatenate([pick(first, idle), pick(second, 0), pick(target, 0)])


def products_kernel(left_count, slots, share, left, right, side, wave, env, keep, send, acc, inter, total):
    inters, rows, dim = acc.shape
    mine, block = side[0], side[1]
    row = 0 if rows == dim else pl.multiple_of(block * rows, rows)
    acc[...] = jnp.zeros_like(acc)
    total[...] = jnp.zeros_like(total)

    @pl.loop(0, left_count // LEFT_UNROLL)
    def _(turn):
        done = []
        for step in range(LEFT_UNROLL):
            at = turn * LEFT_UNROLL + step
            product = jnp.dot(
                env[left[at], pl.ds(row, rows), :],
                wave[left[left_count + at]],
                preferred_element_type=jnp.float32,
            )
            done.append((left[2 * left_count + at], product))
        for place, product in done:
            acc[place] += product

    @pl.loop(0, inters // 8)
    def _(turn):
        for step in range(8):
            inter[turn * 8 + step] = acc[turn * 8 + step].astype(jnp.bfloat16)

    inter[inters] = jnp.zeros((rows, dim), jnp.bfloat16)

    @pl.loop(0, slots // (DEPTH * RIGHT_UNROLL))
    def _(turn):
        done = []
        for step in range(RIGHT_UNROLL):
            base = (turn * RIGHT_UNROLL + step) * DEPTH
            first = [inter[right[base + i]] for i in range(DEPTH)]
            second = [env[right[slots + base + i]] for i in range(DEPTH)]
            product = jnp.dot(
                jnp.concatenate(first, axis=1),
                jnp.concatenate(second, axis=0),
                preferred_element_type=jnp.float32,
            )
            done.append((right[2 * slots + base], product))
        for place, product in done:
            total[place] += product

    parts = rows // share
    keep[...] = total[:, pl.ds(pl.multiple_of(mine * share, share), share), :]
    for hop in range(1, parts):
        other = lax.rem(mine + hop, parts)
        send[hop - 1] = total[:, pl.ds(pl.multiple_of(other * share, share), share), :].astype(
            jnp.bfloat16
        )


def shards(wave_tiles, left_env, right_env, send_list, left_tasks, right_tasks):
    sectors, terms = lax.axis_size("sector"), lax.axis_size("term")
    tiles, vectors, dim, _ = wave_tiles.shape
    term = lax.axis_index("term")
    blocks = terms // vectors
    rows, share = dim // blocks, dim // terms
    vector, block = term % vectors, term // vectors

    vmem = pl.BlockSpec(memory_space=pltpu.VMEM)
    smem = pl.BlockSpec(memory_space=pltpu.SMEM)
    hbm = pl.BlockSpec(memory_space=pl.ANY)
    send_slots = send_list.shape[1]
    outgoing, env = pl.pallas_call(
        functools.partial(pack_kernel, vectors),
        out_shape=(
            jax.ShapeDtypeStruct((send_slots, dim, dim), jnp.bfloat16),
            jax.ShapeDtypeStruct((2, dim, dim), jnp.bfloat16),
        ),
        in_specs=[smem, hbm, hbm, hbm],
        out_specs=(vmem, vmem),
        scratch_shapes=[
            pltpu.VMEM((tiles, dim, dim), jnp.bfloat16),
            pltpu.SemaphoreType.DMA((3,)),
        ],
        name="pack",
    )(send_list, wave_tiles, left_env, right_env)
    env = gather_env(env)
    received = lax.all_to_all(outgoing, "sector", split_axis=0, concat_axis=0, tiled=True)

    tasks = jnp.concatenate([left_tasks[0, 0], right_tasks[0, 0]], axis=0)[None]
    bit = 1
    while bit < terms:
        tasks = jnp.concatenate([tasks, swap(tasks, "term", bit)], axis=0)
        bit *= 2
    left_rows, right_rows = tasks[:, : left_tasks.shape[2]], tasks[:, left_tasks.shape[2] :]
    groups = jnp.arange(terms, dtype=jnp.int32)[:, None] ^ term
    left_count = left_rows.shape[0] * left_rows.shape[1]
    right_count = right_rows.shape[0] * right_rows.shape[1]
    left = jnp.concatenate(
        [
            env_place(groups, left_rows[:, :, 0], 0).reshape(-1),
            left_rows[:, :, 1].reshape(-1),
            (groups * INTER_TILES + left_rows[:, :, 2]).reshape(-1),
        ]
    )
    slots = round_up(right_count + tiles * (DEPTH - 1), DEPTH * RIGHT_UNROLL)
    right = schedule(
        (groups * INTER_TILES + right_rows[:, :, 0]).reshape(-1),
        env_place(groups, right_rows[:, :, 1], 1).reshape(-1),
        right_rows[:, :, 2].reshape(-1),
        tiles,
        DEPTH,
        slots,
        terms * INTER_TILES,
    )
    inters = terms * INTER_TILES
    keep, send = pl.pallas_call(
        functools.partial(products_kernel, left_count, slots, share),
        out_shape=(
            jax.ShapeDtypeStruct((tiles, share, dim), jnp.float32),
            jax.ShapeDtypeStruct((vectors - 1, tiles, share, dim), jnp.bfloat16),
        ),
        in_specs=[smem, smem, smem, vmem, vmem],
        out_specs=(vmem, vmem),
        scratch_shapes=[
            pltpu.VMEM((inters, rows, dim), jnp.float32),
            pltpu.VMEM((inters + 1, rows, dim), jnp.bfloat16),
            pltpu.VMEM((tiles, rows, dim), jnp.float32),
        ],
        compiler_params=pltpu.CompilerParams(vmem_limit_bytes=48 << 20),
        name="products",
    )(left, right, jnp.stack([vector, block]).astype(jnp.int32), received, env)

    pieces = [keep]
    for hop in range(1, vectors):
        pairs = [
            (i, i // vectors * vectors + (i % vectors + hop) % vectors) for i in range(terms)
        ]
        pieces.append(lax.ppermute(send[hop - 1], "term", pairs).astype(jnp.float32))
    hops = (vector - jnp.arange(vectors)[None, :, None, None]) % vectors
    result = pieces[0][:, None]
    for hop in range(1, vectors):
        result = jnp.where(hops == hop, pieces[hop][:, None], result)
    return result


def solution(mesh):
    in_specs = (
        P("sector", None, None, None),
        P("term", "sector", None, None),
        P("term", "sector", None, None),
        P("sector", None),
        P("term", "sector", None, None),
        P("term", "sector", None, None),
    )
    out_specs = P("sector", None, "term", None)
    return jax.shard_map(shards, mesh=mesh, in_specs=in_specs, out_specs=out_specs, check_vma=False)
```

```python
import functools

import jax
import jax.numpy as jnp
from jax import lax
from jax.experimental import pallas as pl
from jax.experimental.pallas import tpu as pltpu
from jax.sharding import PartitionSpec as P

INTER_TILES = 32
PACK_UNROLL = 8
DEPTH = 8
LEFT_UNROLL = 32
RIGHT_UNROLL = 8


def vmem_params(size):
    return pltpu.CompilerParams(vmem_limit_bytes=min(size + (6 << 20), 60 << 20))


def round_up(value, step):
    return -(-value // step) * step


def swap(value, axis, mask):
    size = lax.axis_size(axis)
    return lax.ppermute(value, axis, [(i, i ^ mask) for i in range(size)])


def env_place(group, tile):
    sectors, terms = lax.axis_size("sector"), lax.axis_size("term")
    group = group ^ lax.axis_index("term")
    tile = tile ^ lax.axis_index("sector")
    far = sectors // 4
    place = (tile >> 2) + far * (((tile >> 1) & 1) + 2 * group)
    return place + far * 2 * terms * (tile & 1)


def gather_far(env):
    far = [env]
    far += [swap(env, "sector", mask << 2) for mask in range(1, lax.axis_size("sector") // 4)]
    return jnp.stack(far, axis=1)


def gather_env(column):
    terms = lax.axis_size("term")
    across, over = swap(column, "sector", 2), swap(column, "term", 1)
    corner = jnp.stack([swap(over[0], "sector", 2), swap(across[1], "term", 1)])
    plane = jnp.concatenate([column, across, over, corner], axis=1)
    bit = 2
    while bit < terms:
        plane = jnp.concatenate([plane, swap(plane, "term", bit)], axis=1)
        bit *= 2
    return plane, swap(plane, "sector", 1)


def pack_kernel(vectors, picks, wave, left, right, out, env, held, sems):
    vector = lax.rem(lax.axis_index("term"), vectors)
    copies = [
        pltpu.make_async_copy(wave.at[:, vector], held, sems.at[0]),
        pltpu.make_async_copy(left.at[0, 0], env.at[0], sems.at[1]),
        pltpu.make_async_copy(right.at[0, 0], env.at[1], sems.at[2]),
    ]
    for copy in copies:
        copy.start()
    for copy in copies:
        copy.wait()

    @pl.loop(0, out.shape[0] // PACK_UNROLL)
    def _(turn):
        for step in range(PACK_UNROLL):
            slot = turn * PACK_UNROLL + step
            tile = picks[0, slot]
            picked = held[jnp.maximum(tile, 0)]
            out[slot] = jnp.where(tile >= 0, picked, jnp.zeros_like(picked))


def schedule(first, second, target, targets, depth, turn, slots, idle):
    count = target.shape[0]
    index = jnp.arange(count, dtype=jnp.int32)
    same = target[:, None] == target[None, :]
    rank = jnp.sum(same & (index[None, :] < index[:, None]), axis=1, dtype=jnp.int32)
    names = jnp.arange(targets, dtype=jnp.int32)
    counts = jnp.sum(target[None, :] == names[:, None], axis=1, dtype=jnp.int32)
    padded = (counts + depth - 1) // depth * depth
    starts = jnp.sum(
        jnp.where(names[None, :] < target[:, None], padded[None, :], 0), axis=1, dtype=jnp.int32
    )
    place = starts + rank
    chosen = place[None, :] == jnp.arange(slots, dtype=jnp.int32)[:, None]

    def pick(values, rest):
        return rest + jnp.sum(jnp.where(chosen, values[None, :] - rest, 0), axis=1, dtype=jnp.int32)

    ends = [jnp.sum(padded[: targets // 2]), jnp.sum(padded)]
    turns = [(end + turn - 1) // turn for end in ends]
    return jnp.concatenate([pick(first, idle), pick(second, 0), pick(target, 0)]), turns


def tasks_kernel(left, right, after, out):
    out[...] = jnp.zeros_like(out)
    out[0 : left.shape[0], 0 : left.shape[1]] = left[...]
    out[3 : 3 + right.shape[0], 0 : right.shape[1]] = right[...]


def right_products(right, slots, first_turn, last_turn, inter, env, total):
    @pl.loop(first_turn, last_turn)
    def _(turn):
        done = []
        for step in range(RIGHT_UNROLL):
            base = (turn * RIGHT_UNROLL + step) * DEPTH
            first = [inter[right[base + i]] for i in range(DEPTH)]
            second = [env[right[slots + base + i]] for i in range(DEPTH)]
            product = jnp.dot(
                jnp.concatenate(first, axis=1),
                jnp.concatenate(second, axis=0),
                preferred_element_type=jnp.float32,
            )
            done.append((right[2 * slots + base], product))
        for place, product in done:
            total[place] += product


def give(total, first, count, mine, share, keep, send):
    parts = total.shape[1] // share
    own = pl.ds(pl.multiple_of(mine * share, share), share)
    keep[...] = total[pl.ds(first, count), own, :]
    for hop in range(1, parts):
        other = lax.rem(mine + hop, parts)
        theirs = pl.ds(pl.multiple_of(other * share, share), share)
        send[hop - 1] = total[pl.ds(first, count), theirs, :].astype(jnp.bfloat16)


def first_kernel(
    left_count,
    slots,
    share,
    near,
    left,
    right,
    side,
    wave,
    here,
    there,
    keep,
    send,
    inter,
    env_right,
    rest,
    env_left,
    acc,
    total,
    sems,
):
    inters, rows, dim = acc.shape
    mine, block, middle = side[0], side[1], side[2]
    own = here.shape[1]
    row = pl.ds(0 if rows == dim else pl.multiple_of(block * rows, rows), rows)
    acc[...] = jnp.zeros_like(acc)
    total[...] = jnp.zeros_like(total)
    copies = []
    for place, source in enumerate((here, there)):
        span = pl.ds(place * own, own)
        if near:
            env_left[span] = source[0, :, row]
            env_right[span] = source[1]
            continue
        copies.append(
            pltpu.make_async_copy(source.at[0, :, row], env_left.at[span], sems.at[2 * place])
        )
        copies.append(
            pltpu.make_async_copy(source.at[1], env_right.at[span], sems.at[2 * place + 1])
        )
    for copy in copies:
        copy.start()
    for copy in copies:
        copy.wait()

    @pl.loop(0, left_count // LEFT_UNROLL)
    def _(turn):
        done = []
        for step in range(LEFT_UNROLL):
            at = turn * LEFT_UNROLL + step
            product = jnp.dot(
                env_left[left[at]],
                wave[left[left_count + at]],
                preferred_element_type=jnp.float32,
            )
            done.append((left[2 * left_count + at], product))
        for place, product in done:
            acc[place] += product

    @pl.loop(0, inters // 8)
    def _(turn):
        for step in range(8):
            inter[turn * 8 + step] = acc[turn * 8 + step].astype(jnp.bfloat16)

    inter[inters] = jnp.zeros((rows, dim), jnp.bfloat16)
    right_products(right, slots, 0, middle, inter, env_right, total)
    half = total.shape[0] // 2
    give(total, 0, half, mine, share, keep, send)
    rest[...] = total[half:]


def second_kernel(slots, share, right, side, inter, env, rest, keep, send, total):
    half = rest.shape[0]
    total[half:] = rest[...]
    right_products(right, slots, side[2], side[3], inter, env, total)
    give(total, half, half, side[0], share, keep, send)


def finish_kernel(vectors, first, keep, *rest):
    received, (out, held, sems) = rest[: vectors - 1], rest[-3:]
    count = keep.shape[0]
    vector = lax.rem(lax.axis_index("term"), vectors)
    held[vector] = keep[...]
    for hop in range(1, vectors):
        place = lax.rem(vector + vectors - hop, vectors)
        held[place] = received[hop - 1][...].astype(jnp.float32)
    copies = [
        pltpu.make_async_copy(held.at[i], out.at[pl.ds(first, count), i], sems.at[i])
        for i in range(vectors)
    ]
    for copy in copies:
        copy.start()
    for copy in copies:
        copy.wait()


def finish(keep, received, tiles, first, before=None):
    vectors = len(received) + 1
    count, share, dim = keep.shape
    vmem = pl.BlockSpec(memory_space=pltpu.VMEM)
    hbm = pl.BlockSpec(memory_space=pl.ANY)
    operands = [keep] + received + ([] if before is None else [before])
    return pl.pallas_call(
        functools.partial(finish_kernel, vectors, first),
        out_shape=jax.ShapeDtypeStruct((tiles, vectors, share, dim), jnp.float32),
        in_specs=[vmem] * vectors + ([] if before is None else [hbm]),
        out_specs=hbm,
        scratch_shapes=[
            pltpu.VMEM((vectors, count, share, dim), jnp.float32),
            pltpu.SemaphoreType.DMA((vectors,)),
        ],
        compiler_params=vmem_params(3 * vectors * count * share * dim * 4),
        input_output_aliases={} if before is None else {vectors: 0},
        name="finish",
    )(*operands)


def shards(wave_tiles, left_env, right_env, send_list, left_tasks, right_tasks):
    sectors, terms = lax.axis_size("sector"), lax.axis_size("term")
    tiles, vectors, dim, _ = wave_tiles.shape
    term = lax.axis_index("term")
    blocks = terms // vectors
    rows, share = dim // blocks, dim // terms
    vector, block = term % vectors, term // vectors

    vmem = pl.BlockSpec(memory_space=pltpu.VMEM)
    smem = pl.BlockSpec(memory_space=pltpu.SMEM)
    hbm = pl.BlockSpec(memory_space=pl.ANY)
    send_slots = send_list.shape[1]
    tile_bytes = dim * dim * 2
    outgoing, env = pl.pallas_call(
        functools.partial(pack_kernel, vectors),
        out_shape=(
            jax.ShapeDtypeStruct((send_slots, dim, dim), jnp.bfloat16),
            jax.ShapeDtypeStruct((2, dim, dim), jnp.bfloat16),
        ),
        in_specs=[smem, hbm, hbm, hbm],
        out_specs=(vmem, vmem),
        scratch_shapes=[
            pltpu.VMEM((tiles, dim, dim), jnp.bfloat16),
            pltpu.SemaphoreType.DMA((3,)),
        ],
        compiler_params=vmem_params(54 << 20),
        name="pack",
    )(send_list, wave_tiles, left_env, right_env)
    column = gather_far(env)
    received = lax.all_to_all(outgoing, "sector", split_axis=0, concat_axis=0, tiled=True)
    here, there = gather_env(column)

    left_count, right_count = left_tasks.shape[2], right_tasks.shape[2]
    tasks = pl.pallas_call(
        tasks_kernel,
        out_shape=jax.ShapeDtypeStruct((8, max(left_count, right_count)), jnp.int32),
        in_specs=[vmem, vmem, hbm],
        out_specs=vmem,
        compiler_params=vmem_params(0),
        name="tasks",
    )(left_tasks[0, 0].T, right_tasks[0, 0].T, column)[None]
    bit = 1
    while bit < terms:
        tasks = jnp.concatenate([tasks, swap(tasks, "term", bit)], axis=0)
        bit *= 2
    left_rows, right_rows = tasks[:, 0:3, :left_count], tasks[:, 3:6, :right_count]
    groups = jnp.arange(terms, dtype=jnp.int32)[:, None] ^ term
    left_count, right_count = terms * left_count, terms * right_count
    left = jnp.concatenate(
        [
            env_place(groups, left_rows[:, 0]).reshape(-1),
            left_rows[:, 1].reshape(-1),
            (groups * INTER_TILES + left_rows[:, 2]).reshape(-1),
        ]
    )
    turn = DEPTH * RIGHT_UNROLL
    slots = round_up(right_count + tiles * (DEPTH - 1), turn)
    inters = terms * INTER_TILES
    right, turns = schedule(
        (groups * INTER_TILES + right_rows[:, 0]).reshape(-1),
        env_place(groups, right_rows[:, 1]).reshape(-1),
        right_rows[:, 2].reshape(-1),
        tiles,
        DEPTH,
        turn,
        slots,
        inters,
    )
    side = jnp.stack([vector, block] + turns).astype(jnp.int32)
    half = tiles // 2
    block_bytes = rows * dim * 2
    env_bytes = here.size * 2
    near = env_bytes <= 4 << 20
    rest_bytes = (tiles * 6 + inters) * block_bytes + env_bytes
    first_bytes = rest_bytes + (inters * 2 + here.shape[1] * 2) * block_bytes
    first_bytes += send_slots * tile_bytes + (2 * env_bytes if near else 0)
    keep_shape = jax.ShapeDtypeStruct((half, share, dim), jnp.float32)
    send_shape = jax.ShapeDtypeStruct((vectors - 1, half, share, dim), jnp.bfloat16)
    keep_one, send_one, inter, env_right, rest = pl.pallas_call(
        functools.partial(first_kernel, left_count, slots, share, near),
        out_shape=(
            keep_shape,
            send_shape,
            jax.ShapeDtypeStruct((inters + 1, rows, dim), jnp.bfloat16),
            jax.ShapeDtypeStruct((2 * here.shape[1], dim, dim), jnp.bfloat16),
            jax.ShapeDtypeStruct((tiles - half, rows, dim), jnp.float32),
        ),
        in_specs=[smem, smem, smem, vmem] + [vmem if near else hbm] * 2,
        out_specs=(vmem, vmem, vmem, vmem, vmem),
        scratch_shapes=[
            pltpu.VMEM((2 * here.shape[1], rows, dim), jnp.bfloat16),
            pltpu.VMEM((inters, rows, dim), jnp.float32),
            pltpu.VMEM((tiles, rows, dim), jnp.float32),
            pltpu.SemaphoreType.DMA((4,)),
        ],
        compiler_params=vmem_params(first_bytes),
        name="first_products",
    )(left, right, side, received, here, there)
    keep_two, send_two = pl.pallas_call(
        functools.partial(second_kernel, slots, share),
        out_shape=(keep_shape, send_shape),
        in_specs=[smem, smem, vmem, vmem, vmem],
        out_specs=(vmem, vmem),
        scratch_shapes=[pltpu.VMEM((tiles, rows, dim), jnp.float32)],
        compiler_params=vmem_params(rest_bytes),
        cost_estimate=pl.CostEstimate(
            flops=right_count * rows * dim * dim, bytes_accessed=12 << 20, transcendentals=0
        ),
        name="second_products",
    )(right, side, inter, env_right, rest)

    def exchange(send):
        moved = []
        for hop in range(1, vectors):
            pairs = [
                (i, i // vectors * vectors + (i % vectors + hop) % vectors) for i in range(terms)
            ]
            moved.append(lax.ppermute(send[hop - 1], "term", pairs))
        return moved

    result = finish(keep_one, exchange(send_one), tiles, 0)
    return finish(keep_two, exchange(send_two), tiles, half, result)


def solution(mesh):
    in_specs = (
        P("sector", None, None, None),
        P("term", "sector", None, None),
        P("term", "sector", None, None),
        P("sector", None),
        P("term", "sector", None, None),
        P("term", "sector", None, None),
    )
    out_specs = P("sector", None, "term", None)
    return jax.shard_map(shards, mesh=mesh, in_specs=in_specs, out_specs=out_specs, check_vma=False)
```

```python
import functools

import jax
import jax.numpy as jnp
from jax import lax
from jax.experimental import pallas as pl
from jax.experimental.pallas import tpu as pltpu
from jax.sharding import PartitionSpec as P

INTER_TILES = 32
PACK_UNROLL = 8
DEPTH = 8
LEFT_UNROLL = 32
RIGHT_UNROLL = 8


def vmem_params(size):
    return pltpu.CompilerParams(vmem_limit_bytes=min(size + (6 << 20), 60 << 20))


def round_up(value, step):
    return -(-value // step) * step


def swap(value, axis, mask):
    size = lax.axis_size(axis)
    return lax.ppermute(value, axis, [(i, i ^ mask) for i in range(size)])


def env_place(group, tile):
    sectors, terms = lax.axis_size("sector"), lax.axis_size("term")
    group = group ^ lax.axis_index("term")
    tile = tile ^ lax.axis_index("sector")
    far = sectors // 4
    place = (tile >> 2) + far * (((tile >> 1) & 1) + 2 * group)
    return place + far * 2 * terms * (tile & 1)


def column_kernel(count, *refs):
    tiles, sides = refs[:count], refs[count:]
    for place in range(count):
        for side in range(2):
            sides[side][place] = tiles[place][side]


def gather_far(env):
    count = lax.axis_size("sector") // 4
    vmem = pl.BlockSpec(memory_space=pltpu.VMEM)
    return pl.pallas_call(
        functools.partial(column_kernel, count),
        out_shape=[jax.ShapeDtypeStruct((count,) + env.shape[1:], env.dtype)] * 2,
        in_specs=[vmem] * count,
        out_specs=[vmem] * 2,
        compiler_params=vmem_params(4 * count * env.size),
        name="column",
    )(env, *[swap(env, "sector", mask << 2) for mask in range(1, count)])


def gather_env(column):
    terms = lax.axis_size("term")
    sides = []
    for side in range(2):
        across, over = swap(column[side], "sector", 2), swap(column[side], "term", 1)
        plane = jnp.concatenate([column[side], across, over, swap(across, "term", 1)])
        bit = 2
        while bit < terms:
            plane = jnp.concatenate([plane, swap(plane, "term", bit)])
            bit *= 2
        sides.append((plane, swap(plane, "sector", 1)))
    return sides


def pack_kernel(vectors, picks, wave, left, right, out, env, held, sems):
    vector = lax.rem(lax.axis_index("term"), vectors)
    copies = [
        pltpu.make_async_copy(wave.at[:, vector], held, sems.at[0]),
        pltpu.make_async_copy(left.at[0, 0], env.at[0], sems.at[1]),
        pltpu.make_async_copy(right.at[0, 0], env.at[1], sems.at[2]),
    ]
    for copy in copies:
        copy.start()
    for copy in copies:
        copy.wait()

    @pl.loop(0, out.shape[0] // PACK_UNROLL)
    def _(turn):
        for step in range(PACK_UNROLL):
            slot = turn * PACK_UNROLL + step
            tile = picks[0, slot]
            picked = held[jnp.maximum(tile, 0)]
            out[slot] = jnp.where(tile >= 0, picked, jnp.zeros_like(picked))


def schedule(first, second, target, targets, middle, depth, turn, slots, idle):
    count = target.shape[0]
    index = jnp.arange(count, dtype=jnp.int32)
    same = target[:, None] == target[None, :]
    rank = jnp.sum(same & (index[None, :] < index[:, None]), axis=1, dtype=jnp.int32)
    names = jnp.arange(targets, dtype=jnp.int32)
    counts = jnp.sum(target[None, :] == names[:, None], axis=1, dtype=jnp.int32)
    padded = (counts + depth - 1) // depth * depth
    starts = jnp.sum(
        jnp.where(names[None, :] < target[:, None], padded[None, :], 0), axis=1, dtype=jnp.int32
    )
    place = starts + rank
    chosen = place[None, :] == jnp.arange(slots, dtype=jnp.int32)[:, None]

    def pick(values, rest):
        return rest + jnp.sum(jnp.where(chosen, values[None, :] - rest, 0), axis=1, dtype=jnp.int32)

    ends = [jnp.sum(padded[:middle]), jnp.sum(padded)]
    turns = [(end + turn - 1) // turn for end in ends]
    return jnp.concatenate([pick(first, idle), pick(second, 0), pick(target, 0)]), turns


def tasks_kernel(left, right, after, out):
    out[...] = jnp.zeros_like(out)
    out[0 : left.shape[0], 0 : left.shape[1]] = left[...]
    out[3 : 3 + right.shape[0], 0 : right.shape[1]] = right[...]


def right_products(right, slots, first_turn, last_turn, inter, env, total):
    @pl.loop(first_turn, last_turn)
    def _(turn):
        done = []
        for step in range(RIGHT_UNROLL):
            base = (turn * RIGHT_UNROLL + step) * DEPTH
            first = [inter[right[base + i]] for i in range(DEPTH)]
            second = [env[right[slots + base + i]] for i in range(DEPTH)]
            product = jnp.dot(
                jnp.concatenate(first, axis=1),
                jnp.concatenate(second, axis=0),
                preferred_element_type=jnp.float32,
            )
            done.append((right[2 * slots + base], product))
        for place, product in done:
            total[place] += product


def give(total, first, count, mine, share, keep, send):
    parts = total.shape[1] // share
    own = pl.ds(pl.multiple_of(mine * share, share), share)
    keep[...] = total[pl.ds(first, count), own, :]
    for hop in range(1, parts):
        other = lax.rem(mine + hop, parts)
        theirs = pl.ds(pl.multiple_of(other * share, share), share)
        send[hop - 1] = total[pl.ds(first, count), theirs, :].astype(jnp.bfloat16)


def join(near, pieces, row, out, sems):
    copies = []
    for place, piece in enumerate(pieces):
        span = pl.ds(place * piece.shape[0], piece.shape[0])
        if near:
            out[span] = piece[:, row]
        else:
            copies.append(pltpu.make_async_copy(piece.at[:, row], out.at[span], sems.at[place]))
    for copy in copies:
        copy.start()
    for copy in copies:
        copy.wait()


def left_kernel(count, near, left, side, wave, here, there, inter, env, acc, sems):
    inters, rows, dim = acc.shape
    first_row = 0 if rows == dim else pl.multiple_of(side[1] * rows, rows)
    acc[...] = jnp.zeros_like(acc)
    join(near, (here, there), pl.ds(first_row, rows), env, sems)

    @pl.loop(0, count // LEFT_UNROLL)
    def _(turn):
        done = []
        for step in range(LEFT_UNROLL):
            at = turn * LEFT_UNROLL + step
            product = jnp.dot(
                env[left[at]], wave[left[count + at]], preferred_element_type=jnp.float32
            )
            done.append((left[2 * count + at], product))
        for place, product in done:
            acc[place] += product

    @pl.loop(0, inters // 8)
    def _(turn):
        for step in range(8):
            inter[turn * 8 + step] = acc[turn * 8 + step].astype(jnp.bfloat16)

    inter[inters] = jnp.zeros((rows, dim), jnp.bfloat16)


def first_kernel(
    slots, share, near, right, side, inter, here, there, keep, send, env, rest, total, sems
):
    total[...] = jnp.zeros_like(total)
    join(near, (here, there), pl.ds(0, here.shape[1]), env, sems)
    right_products(right, slots, 0, side[2], inter, env, total)
    middle = keep.shape[0]
    give(total, 0, middle, side[0], share, keep, send)
    rest[...] = total[middle:]


def second_kernel(slots, share, right, side, inter, env, rest, keep, send, total):
    count = rest.shape[0]
    middle = total.shape[0] - count
    total[middle:] = rest[...]
    right_products(right, slots, side[2], side[3], inter, env, total)
    give(total, middle, count, side[0], share, keep, send)


def finish_kernel(vectors, first, keep, *rest):
    received, (out, held, sems) = rest[: vectors - 1], rest[-3:]
    count = keep.shape[0]
    vector = lax.rem(lax.axis_index("term"), vectors)
    held[vector] = keep[...]
    for hop in range(1, vectors):
        place = lax.rem(vector + vectors - hop, vectors)
        held[place] = received[hop - 1][...].astype(jnp.float32)
    copies = [
        pltpu.make_async_copy(held.at[i], out.at[pl.ds(first, count), i], sems.at[i])
        for i in range(vectors)
    ]
    for copy in copies:
        copy.start()
    for copy in copies:
        copy.wait()


def finish(keep, received, tiles, first, before=None):
    vectors = len(received) + 1
    count, share, dim = keep.shape
    vmem = pl.BlockSpec(memory_space=pltpu.VMEM)
    hbm = pl.BlockSpec(memory_space=pl.ANY)
    operands = [keep] + received + ([] if before is None else [before])
    return pl.pallas_call(
        functools.partial(finish_kernel, vectors, first),
        out_shape=jax.ShapeDtypeStruct((tiles, vectors, share, dim), jnp.float32),
        in_specs=[vmem] * vectors + ([] if before is None else [hbm]),
        out_specs=hbm,
        scratch_shapes=[
            pltpu.VMEM((vectors, count, share, dim), jnp.float32),
            pltpu.SemaphoreType.DMA((vectors,)),
        ],
        compiler_params=vmem_params(3 * vectors * count * share * dim * 4),
        input_output_aliases={} if before is None else {vectors: 0},
        name="finish",
    )(*operands)


def shards(wave_tiles, left_env, right_env, send_list, left_tasks, right_tasks):
    sectors, terms = lax.axis_size("sector"), lax.axis_size("term")
    tiles, vectors, dim, _ = wave_tiles.shape
    term = lax.axis_index("term")
    blocks = terms // vectors
    rows, share = dim // blocks, dim // terms
    vector, block = term % vectors, term // vectors

    vmem = pl.BlockSpec(memory_space=pltpu.VMEM)
    smem = pl.BlockSpec(memory_space=pltpu.SMEM)
    hbm = pl.BlockSpec(memory_space=pl.ANY)
    send_slots = send_list.shape[1]
    tile_bytes = dim * dim * 2
    outgoing, env = pl.pallas_call(
        functools.partial(pack_kernel, vectors),
        out_shape=(
            jax.ShapeDtypeStruct((send_slots, dim, dim), jnp.bfloat16),
            jax.ShapeDtypeStruct((2, dim, dim), jnp.bfloat16),
        ),
        in_specs=[smem, hbm, hbm, hbm],
        out_specs=(vmem, vmem),
        scratch_shapes=[
            pltpu.VMEM((tiles, dim, dim), jnp.bfloat16),
            pltpu.SemaphoreType.DMA((3,)),
        ],
        compiler_params=vmem_params(54 << 20),
        name="pack",
    )(send_list, wave_tiles, left_env, right_env)
    column = gather_far(env)
    received = lax.all_to_all(outgoing, "sector", split_axis=0, concat_axis=0, tiled=True)
    sides = gather_env(column)

    left_count, right_count = left_tasks.shape[2], right_tasks.shape[2]
    tasks = pl.pallas_call(
        tasks_kernel,
        out_shape=jax.ShapeDtypeStruct((8, max(left_count, right_count)), jnp.int32),
        in_specs=[vmem, vmem, hbm],
        out_specs=vmem,
        compiler_params=vmem_params(0),
        name="tasks",
    )(left_tasks[0, 0].T, right_tasks[0, 0].T, column[0])[None]
    bit = 1
    while bit < terms:
        tasks = jnp.concatenate([tasks, swap(tasks, "term", bit)], axis=0)
        bit *= 2
    left_rows, right_rows = tasks[:, 0:3, :left_count], tasks[:, 3:6, :right_count]
    groups = jnp.arange(terms, dtype=jnp.int32)[:, None] ^ term
    left_count, right_count = terms * left_count, terms * right_count
    left = jnp.concatenate(
        [
            env_place(groups, left_rows[:, 0]).reshape(-1),
            left_rows[:, 1].reshape(-1),
            (groups * INTER_TILES + left_rows[:, 2]).reshape(-1),
        ]
    )
    turn = DEPTH * RIGHT_UNROLL
    middle = tiles * 3 // 4
    slots = round_up(right_count + tiles * (DEPTH - 1), turn)
    inters = terms * INTER_TILES
    right, turns = schedule(
        (groups * INTER_TILES + right_rows[:, 0]).reshape(-1),
        env_place(groups, right_rows[:, 1]).reshape(-1),
        right_rows[:, 2].reshape(-1),
        tiles,
        middle,
        DEPTH,
        turn,
        slots,
        inters,
    )
    side = jnp.stack([vector, block] + turns).astype(jnp.int32)
    block_bytes = rows * dim * 2
    env_tiles = terms * sectors
    env_bytes = env_tiles * tile_bytes
    near = env_bytes <= 2 << 20
    env_spec = vmem if near else hbm
    left_bytes = send_slots * tile_bytes + (3 * inters + env_tiles) * block_bytes
    right_bytes = (tiles * 6 + inters) * block_bytes + env_bytes
    inter = pl.pallas_call(
        functools.partial(left_kernel, left_count, near),
        out_shape=jax.ShapeDtypeStruct((inters + 1, rows, dim), jnp.bfloat16),
        in_specs=[smem, smem, vmem, env_spec, env_spec],
        out_specs=vmem,
        scratch_shapes=[
            pltpu.VMEM((env_tiles, rows, dim), jnp.bfloat16),
            pltpu.VMEM((inters, rows, dim), jnp.float32),
            pltpu.SemaphoreType.DMA((2,)),
        ],
        compiler_params=vmem_params(left_bytes + near * env_bytes),
        cost_estimate=pl.CostEstimate(
            flops=2 * left_count * rows * dim * dim, bytes_accessed=8 << 20, transcendentals=0
        ),
        name="left_products",
    )(left, side, received, *sides[0])

    def sigma_shapes(count):
        return (
            jax.ShapeDtypeStruct((count, share, dim), jnp.float32),
            jax.ShapeDtypeStruct((vectors - 1, count, share, dim), jnp.bfloat16),
        )

    keep_one, send_one, env_right, rest = pl.pallas_call(
        functools.partial(first_kernel, slots, share, near),
        out_shape=sigma_shapes(middle)
        + (
            jax.ShapeDtypeStruct((env_tiles, dim, dim), jnp.bfloat16),
            jax.ShapeDtypeStruct((tiles - middle, rows, dim), jnp.float32),
        ),
        in_specs=[smem, smem, vmem, env_spec, env_spec],
        out_specs=(vmem, vmem, vmem, vmem),
        scratch_shapes=[
            pltpu.VMEM((tiles, rows, dim), jnp.float32),
            pltpu.SemaphoreType.DMA((2,)),
        ],
        compiler_params=vmem_params(right_bytes + near * env_bytes),
        name="first_products",
    )(right, side, inter, *sides[1])
    keep_two, send_two = pl.pallas_call(
        functools.partial(second_kernel, slots, share),
        out_shape=sigma_shapes(tiles - middle),
        in_specs=[smem, smem, vmem, vmem, vmem],
        out_specs=(vmem, vmem),
        scratch_shapes=[pltpu.VMEM((tiles, rows, dim), jnp.float32)],
        compiler_params=vmem_params(right_bytes),
        cost_estimate=pl.CostEstimate(
            flops=right_count * rows * dim * dim, bytes_accessed=12 << 20, transcendentals=0
        ),
        name="second_products",
    )(right, side, inter, env_right, rest)

    def exchange(send):
        moved = []
        for hop in range(1, vectors):
            pairs = [
                (i, i // vectors * vectors + (i % vectors + hop) % vectors) for i in range(terms)
            ]
            moved.append(lax.ppermute(send[hop - 1], "term", pairs))
        return moved

    result = finish(keep_one, exchange(send_one), tiles, 0)
    return finish(keep_two, exchange(send_two), tiles, middle, result)


def solution(mesh):
    in_specs = (
        P("sector", None, None, None),
        P("term", "sector", None, None),
        P("term", "sector", None, None),
        P("sector", None),
        P("term", "sector", None, None),
        P("term", "sector", None, None),
    )
    out_specs = P("sector", None, "term", None)
    return jax.shard_map(shards, mesh=mesh, in_specs=in_specs, out_specs=out_specs, check_vma=False)
```

```python
import functools

import jax
import jax.numpy as jnp
from jax import lax
from jax.experimental import pallas as pl
from jax.experimental.pallas import tpu as pltpu
from jax.sharding import PartitionSpec as P

INTER_TILES = 32
PACK_UNROLL = 8
DEPTH = 8
LEFT_UNROLL = 32
RIGHT_UNROLL = 8


def vmem_params(size):
    return pltpu.CompilerParams(vmem_limit_bytes=min(size + (6 << 20), 60 << 20))


def round_up(value, step):
    return -(-value // step) * step


def swap(value, axis, mask):
    size = lax.axis_size(axis)
    return lax.ppermute(value, axis, [(i, i ^ mask) for i in range(size)])


def env_place(group, tile):
    sectors, terms = lax.axis_size("sector"), lax.axis_size("term")
    group = group ^ lax.axis_index("term")
    tile = tile ^ lax.axis_index("sector")
    far = sectors // 4
    place = (tile >> 2) + far * (((tile >> 1) & 1) + 2 * group)
    return place + far * 2 * terms * (tile & 1)


def column_kernel(count, *refs):
    tiles, sides = refs[:count], refs[count:]
    for place in range(count):
        for side in range(2):
            sides[side][place] = tiles[place][side]


def gather_far(env):
    count = lax.axis_size("sector") // 4
    vmem = pl.BlockSpec(memory_space=pltpu.VMEM)
    return pl.pallas_call(
        functools.partial(column_kernel, count),
        out_shape=[jax.ShapeDtypeStruct((count,) + env.shape[1:], env.dtype)] * 2,
        in_specs=[vmem] * count,
        out_specs=[vmem] * 2,
        compiler_params=vmem_params(4 * count * env.size),
        name="column",
    )(env, *[swap(env, "sector", mask << 2) for mask in range(1, count)])


def gather_env(column):
    terms = lax.axis_size("term")
    sides = []
    for side in range(2):
        across, over = swap(column[side], "sector", 2), swap(column[side], "term", 1)
        plane = jnp.concatenate([column[side], across, over, swap(across, "term", 1)])
        bit = 2
        while bit < terms:
            plane = jnp.concatenate([plane, swap(plane, "term", bit)])
            bit *= 2
        sides.append((plane, swap(plane, "sector", 1)))
    return sides


def pack_kernel(vectors, listed, wave, left, right, out, env, held, picks, sems):
    vector = lax.rem(lax.axis_index("term"), vectors)
    copies = [
        pltpu.make_async_copy(wave.at[:, vector], held, sems.at[0]),
        pltpu.make_async_copy(left.at[0, 0], env.at[0], sems.at[1]),
        pltpu.make_async_copy(right.at[0, 0], env.at[1], sems.at[2]),
        pltpu.make_async_copy(listed, picks, sems.at[3]),
    ]
    for copy in copies:
        copy.start()
    copies[0].wait()
    copies[3].wait()

    @pl.loop(0, out.shape[0] // PACK_UNROLL)
    def _(turn):
        for step in range(PACK_UNROLL):
            slot = turn * PACK_UNROLL + step
            tile = picks[0, slot]
            picked = held[jnp.maximum(tile, 0)]
            out[slot] = jnp.where(tile >= 0, picked, jnp.zeros_like(picked))

    copies[1].wait()
    copies[2].wait()


def schedule(first, second, target, targets, depth, turn, slots, idle):
    count = target.shape[0]
    index = jnp.arange(count, dtype=jnp.int32)
    same = target[:, None] == target[None, :]
    rank = jnp.sum(same & (index[None, :] < index[:, None]), axis=1, dtype=jnp.int32)
    names = jnp.arange(targets, dtype=jnp.int32)
    counts = jnp.sum(target[None, :] == names[:, None], axis=1, dtype=jnp.int32)
    padded = (counts + depth - 1) // depth * depth
    starts = jnp.sum(
        jnp.where(names[None, :] < target[:, None], padded[None, :], 0), axis=1, dtype=jnp.int32
    )
    place = starts + rank
    chosen = place[None, :] == jnp.arange(slots, dtype=jnp.int32)[:, None]

    def pick(values, rest):
        return rest + jnp.sum(jnp.where(chosen, values[None, :] - rest, 0), axis=1, dtype=jnp.int32)

    turns = (jnp.sum(padded) + turn - 1) // turn
    return jnp.concatenate([pick(first, idle), pick(second, 0), pick(target, 0), turns[None]])


def tasks_kernel(left, right, after, out):
    out[...] = jnp.zeros_like(out)
    out[0 : left.shape[0], 0 : left.shape[1]] = left[...]
    out[3 : 3 + right.shape[0], 0 : right.shape[1]] = right[...]


def right_products(right, slots, row, inter, env, total):
    rows = pl.ds(row, total.shape[1])

    @pl.loop(0, right[3 * slots])
    def _(turn):
        done = []
        for step in range(RIGHT_UNROLL):
            base = (turn * RIGHT_UNROLL + step) * DEPTH
            first = [inter[right[base + i], rows, :] for i in range(DEPTH)]
            second = [env[right[slots + base + i]] for i in range(DEPTH)]
            product = jnp.dot(
                jnp.concatenate(first, axis=1),
                jnp.concatenate(second, axis=0),
                preferred_element_type=jnp.float32,
            )
            done.append((right[2 * slots + base], product))
        for place, product in done:
            total[place] += product


def join(near, pieces, row, out, sems):
    copies = []
    for place, piece in enumerate(pieces):
        span = pl.ds(place * piece.shape[0], piece.shape[0])
        if near:
            out[span] = piece[:, row]
        else:
            copies.append(pltpu.make_async_copy(piece.at[:, row], out.at[span], sems.at[place]))
    for copy in copies:
        copy.start()
    for copy in copies:
        copy.wait()


def left_kernel(count, vectors, near, listed, wave, here, there, inter, env, acc, left, sems):
    inters, rows, dim = acc.shape
    lists = pltpu.make_async_copy(listed, left, sems.at[2])
    lists.start()
    first_row = 0
    if rows < dim:
        first_row = pl.multiple_of(lax.div(lax.axis_index("term"), vectors) * rows, rows)
    acc[...] = jnp.zeros_like(acc)
    join(near, (here, there), pl.ds(first_row, rows), env, sems)
    lists.wait()

    @pl.loop(0, count // LEFT_UNROLL)
    def _(turn):
        done = []
        for step in range(LEFT_UNROLL):
            at = turn * LEFT_UNROLL + step
            product = jnp.dot(
                env[left[at]], wave[left[count + at]], preferred_element_type=jnp.float32
            )
            done.append((left[2 * count + at], product))
        for place, product in done:
            acc[place] += product

    @pl.loop(0, inters // 8)
    def _(turn):
        for step in range(8):
            inter[turn * 8 + step] = acc[turn * 8 + step].astype(jnp.bfloat16)

    inter[inters] = jnp.zeros((rows, dim), jnp.bfloat16)


def theirs_kernel(slots, near, listed, inter, here, there, send, env, total, right, sems):
    lists = pltpu.make_async_copy(listed, right, sems.at[2])
    lists.start()
    join(near, (here, there), pl.ds(0, here.shape[1]), env, sems)
    total[...] = jnp.zeros_like(total)
    lists.wait()
    parts, share = send.shape[0] + 1, total.shape[1]
    vector = lax.rem(lax.axis_index("term"), parts)
    for hop in range(1, parts):
        if hop > 1:
            total[...] = jnp.zeros_like(total)
        part = lax.rem(vector + hop, parts)
        row = pl.multiple_of(part * share, share)
        right_products(right, slots, row, inter, env, total)
        send[hop - 1] = total[...].astype(jnp.bfloat16)


def own_kernel(slots, listed, inter, env, out, total, right, sems):
    lists = pltpu.make_async_copy(listed, right, sems.at[0])
    lists.start()
    total[...] = jnp.zeros_like(total)
    lists.wait()
    share = total.shape[1]
    vector = lax.rem(lax.axis_index("term"), out.shape[1])
    row = pl.multiple_of(vector * share, share)
    right_products(right, slots, row, inter, env, total)
    copy = pltpu.make_async_copy(total, out.at[:, vector], sems.at[1])
    copy.start()
    copy.wait()


def finish_kernel(vectors, *refs):
    received, (_, out, held, sems) = refs[: vectors - 1], refs[vectors - 1 :]
    vector = lax.rem(lax.axis_index("term"), vectors)
    copies = []
    for hop in range(1, vectors):
        held[hop - 1] = received[hop - 1][...].astype(jnp.float32)
        place = lax.rem(vector + vectors - hop, vectors)
        copies.append(
            pltpu.make_async_copy(held.at[hop - 1], out.at[:, place], sems.at[hop - 1])
        )
        copies[-1].start()
    for copy in copies:
        copy.wait()


def shards(wave_tiles, left_env, right_env, send_list, left_tasks, right_tasks):
    sectors, terms = lax.axis_size("sector"), lax.axis_size("term")
    tiles, vectors, dim, _ = wave_tiles.shape
    term = lax.axis_index("term")
    blocks = terms // vectors
    rows, share = dim // blocks, dim // terms
    vector, block = term % vectors, term // vectors

    vmem = pl.BlockSpec(memory_space=pltpu.VMEM)
    hbm = pl.BlockSpec(memory_space=pl.ANY)
    send_slots = send_list.shape[1]
    tile_bytes = dim * dim * 2
    outgoing, env = pl.pallas_call(
        functools.partial(pack_kernel, vectors),
        out_shape=(
            jax.ShapeDtypeStruct((send_slots, dim, dim), jnp.bfloat16),
            jax.ShapeDtypeStruct((2, dim, dim), jnp.bfloat16),
        ),
        in_specs=[hbm, hbm, hbm, hbm],
        out_specs=(vmem, vmem),
        scratch_shapes=[
            pltpu.VMEM((tiles, dim, dim), jnp.bfloat16),
            pltpu.SMEM(send_list.shape, jnp.int32),
            pltpu.SemaphoreType.DMA((4,)),
        ],
        compiler_params=vmem_params(54 << 20),
        name="pack",
    )(send_list, wave_tiles, left_env, right_env)
    column = gather_far(env)
    received = lax.all_to_all(outgoing, "sector", split_axis=0, concat_axis=0, tiled=True)
    sides = gather_env(column)

    left_count, right_count = left_tasks.shape[2], right_tasks.shape[2]
    tasks = pl.pallas_call(
        tasks_kernel,
        out_shape=jax.ShapeDtypeStruct((8, max(left_count, right_count)), jnp.int32),
        in_specs=[vmem, vmem, hbm],
        out_specs=vmem,
        compiler_params=vmem_params(0),
        name="tasks",
    )(left_tasks[0, 0].T, right_tasks[0, 0].T, column[0])[None]
    bit = 1
    while bit < terms:
        tasks = jnp.concatenate([tasks, swap(tasks, "term", bit)], axis=0)
        bit *= 2
    left_rows, right_rows = tasks[:, 0:3, :left_count], tasks[:, 3:6, :right_count]
    groups = jnp.arange(terms, dtype=jnp.int32)[:, None] ^ term
    left_count, right_count = terms * left_count, terms * right_count
    left = jnp.concatenate(
        [
            env_place(groups, left_rows[:, 0]).reshape(-1),
            left_rows[:, 1].reshape(-1),
            (groups * INTER_TILES + left_rows[:, 2]).reshape(-1),
        ]
    )
    turn = DEPTH * RIGHT_UNROLL
    slots = round_up(right_count + tiles * (DEPTH - 1), turn)
    inters = terms * INTER_TILES
    right = schedule(
        (groups * INTER_TILES + right_rows[:, 0]).reshape(-1),
        env_place(groups, right_rows[:, 1]).reshape(-1),
        right_rows[:, 2].reshape(-1),
        tiles,
        DEPTH,
        turn,
        slots,
        inters,
    )
    block_bytes = rows * dim * 2
    env_tiles = terms * sectors
    env_bytes = env_tiles * tile_bytes
    near = env_bytes <= 2 << 20
    env_spec = vmem if near else hbm
    left_bytes = send_slots * tile_bytes + (3 * inters + env_tiles) * block_bytes
    right_bytes = (tiles * 2 + inters) * block_bytes + env_bytes
    inter = pl.pallas_call(
        functools.partial(left_kernel, left_count, vectors, near),
        out_shape=jax.ShapeDtypeStruct((inters + 1, rows, dim), jnp.bfloat16),
        in_specs=[hbm, vmem, env_spec, env_spec],
        out_specs=vmem,
        scratch_shapes=[
            pltpu.VMEM((env_tiles, rows, dim), jnp.bfloat16),
            pltpu.VMEM((inters, rows, dim), jnp.float32),
            pltpu.SMEM(left.shape, jnp.int32),
            pltpu.SemaphoreType.DMA((3,)),
        ],
        compiler_params=vmem_params(left_bytes + near * env_bytes),
        cost_estimate=pl.CostEstimate(
            flops=2 * left_count * rows * dim * dim, bytes_accessed=8 << 20, transcendentals=0
        ),
        name="left_products",
    )(left, received, *sides[0])
    send, env_right = pl.pallas_call(
        functools.partial(theirs_kernel, slots, near),
        out_shape=(
            jax.ShapeDtypeStruct((vectors - 1, tiles, share, dim), jnp.bfloat16),
            jax.ShapeDtypeStruct((env_tiles, dim, dim), jnp.bfloat16),
        ),
        in_specs=[hbm, vmem, env_spec, env_spec],
        out_specs=(vmem, vmem),
        scratch_shapes=[
            pltpu.VMEM((tiles, share, dim), jnp.float32),
            pltpu.SMEM(right.shape, jnp.int32),
            pltpu.SemaphoreType.DMA((3,)),
        ],
        compiler_params=vmem_params(right_bytes + near * env_bytes),
        name="their_products",
    )(right, inter, *sides[1])
    result = pl.pallas_call(
        functools.partial(own_kernel, slots),
        out_shape=jax.ShapeDtypeStruct((tiles, vectors, share, dim), jnp.float32),
        in_specs=[hbm, vmem, vmem],
        out_specs=hbm,
        scratch_shapes=[
            pltpu.VMEM((tiles, share, dim), jnp.float32),
            pltpu.SMEM(right.shape, jnp.int32),
            pltpu.SemaphoreType.DMA((2,)),
        ],
        compiler_params=vmem_params(right_bytes),
        cost_estimate=pl.CostEstimate(
            flops=2 * right_count * share * dim * dim, bytes_accessed=12 << 20, transcendentals=0
        ),
        name="own_products",
    )(right, inter, env_right)
    moved = []
    for hop in range(1, vectors):
        pairs = [
            (i, i // vectors * vectors + (i % vectors + hop) % vectors) for i in range(terms)
        ]
        moved.append(lax.ppermute(send[hop - 1], "term", pairs))
    return pl.pallas_call(
        functools.partial(finish_kernel, vectors),
        out_shape=jax.ShapeDtypeStruct((tiles, vectors, share, dim), jnp.float32),
        in_specs=[vmem] * (vectors - 1) + [hbm],
        out_specs=hbm,
        scratch_shapes=[
            pltpu.VMEM((vectors - 1, tiles, share, dim), jnp.float32),
            pltpu.SemaphoreType.DMA((vectors - 1,)),
        ],
        compiler_params=vmem_params(2 * vectors * tiles * share * dim * 4),
        input_output_aliases={vectors - 1: 0},
        name="finish",
    )(*moved, result)


def solution(mesh):
    in_specs = (
        P("sector", None, None, None),
        P("term", "sector", None, None),
        P("term", "sector", None, None),
        P("sector", None),
        P("term", "sector", None, None),
        P("term", "sector", None, None),
    )
    out_specs = P("sector", None, "term", None)
    return jax.shard_map(shards, mesh=mesh, in_specs=in_specs, out_specs=out_specs, check_vma=False)
```

```python
import functools

import jax
import jax.numpy as jnp
from jax import lax
from jax.experimental import pallas as pl
from jax.experimental.pallas import tpu as pltpu
from jax.sharding import PartitionSpec as P

INTER_TILES = 32
PACK_UNROLL = 8
DEPTH = 8
LEFT_UNROLL = 64
RIGHT_UNROLL = 4


def vmem_params(size):
    return pltpu.CompilerParams(vmem_limit_bytes=min(size + (6 << 20), 60 << 20))


def round_up(value, step):
    return -(-value // step) * step


def swap(value, axis, mask):
    size = lax.axis_size(axis)
    return lax.ppermute(value, axis, [(i, i ^ mask) for i in range(size)])


def cross(value, first):
    sectors, terms = lax.axis_size("sector"), lax.axis_size("term")
    pairs = []
    for i in range(terms * sectors):
        pairs.append((i, i ^ (sectors if (i & 1) == first else 2)))
    return lax.ppermute(value, ("term", "sector"), pairs)


def env_place(group, tile):
    sectors, terms = lax.axis_size("sector"), lax.axis_size("term")
    core = tile & 1
    group = group ^ lax.axis_index("term")
    tile = tile ^ lax.axis_index("sector")
    far = sectors // 4
    over, across = group & 1, (tile >> 1) & 1
    square = jnp.where(core == 0, over + 2 * across, across + 2 * over)
    place = (tile >> 2) + far * (square + 4 * (group >> 1))
    return place + far * 2 * terms * (tile & 1)


def column_kernel(count, *refs):
    tiles, sides = refs[:count], refs[count:]
    for place in range(count):
        for side in range(2):
            sides[side][place] = tiles[place][side]


def gather_far(env):
    count = lax.axis_size("sector") // 4
    vmem = pl.BlockSpec(memory_space=pltpu.VMEM)
    return pl.pallas_call(
        functools.partial(column_kernel, count),
        out_shape=[jax.ShapeDtypeStruct((count,) + env.shape[1:], env.dtype)] * 2,
        in_specs=[vmem] * count,
        out_specs=[vmem] * 2,
        compiler_params=vmem_params(4 * count * env.size),
        name="column",
    )(env, *[swap(env, "sector", mask << 2) for mask in range(1, count)])


def gather_env(column):
    terms = lax.axis_size("term")
    sides = []
    for side in range(2):
        one, two = cross(column[side], 0), cross(column[side], 1)
        plane = jnp.concatenate([column[side], one, two, cross(one, 1)])
        bit = 2
        while bit < terms:
            plane = jnp.concatenate([plane, swap(plane, "term", bit)])
            bit *= 2
        sides.append((plane, swap(plane, "sector", 1)))
    return sides


def pack_kernel(vectors, listed, wave, left, right, out, env, held, picks, sems):
    vector = lax.rem(lax.axis_index("term"), vectors)
    copies = [
        pltpu.make_async_copy(wave.at[:, vector], held, sems.at[0]),
        pltpu.make_async_copy(left.at[0, 0], env.at[0], sems.at[1]),
        pltpu.make_async_copy(right.at[0, 0], env.at[1], sems.at[2]),
        pltpu.make_async_copy(listed, picks, sems.at[3]),
    ]
    for copy in copies:
        copy.start()
    copies[0].wait()
    copies[3].wait()

    @pl.loop(0, out.shape[0] // PACK_UNROLL)
    def _(turn):
        for step in range(PACK_UNROLL):
            slot = turn * PACK_UNROLL + step
            tile = picks[0, slot]
            picked = held[jnp.maximum(tile, 0)]
            out[slot] = jnp.where(tile >= 0, picked, jnp.zeros_like(picked))

    copies[1].wait()
    copies[2].wait()


def schedule(first, second, target, targets, cut, depth, turn, slots, idle):
    count = target.shape[0]
    index = jnp.arange(count, dtype=jnp.int32)
    same = target[:, None] == target[None, :]
    rank = jnp.sum(same & (index[None, :] < index[:, None]), axis=1, dtype=jnp.int32)
    names = jnp.arange(targets, dtype=jnp.int32)
    counts = jnp.sum(target[None, :] == names[:, None], axis=1, dtype=jnp.int32)
    padded = (counts + depth - 1) // depth * depth

    def before(bounds):
        lower = names[None, :] < bounds[:, None]
        return jnp.sum(jnp.where(lower, padded[None, :], 0), axis=1, dtype=jnp.int32)

    head = before(jnp.full((targets,), cut, jnp.int32))
    padded = padded + jnp.where(names == cut - 1, -head & (turn - 1), 0)
    starts = before(target)
    place = starts + rank
    chosen = place[None, :] == jnp.arange(slots, dtype=jnp.int32)[:, None]

    def pick(values, rest):
        return rest + jnp.sum(jnp.where(chosen, values[None, :] - rest, 0), axis=1, dtype=jnp.int32)

    ends = before(cut + (targets - cut) * jnp.arange(2, dtype=jnp.int32))
    return jnp.concatenate([pick(first, idle), pick(second, 0), pick(target, cut), ends])


def tasks_kernel(left, right, after, out):
    out[...] = jnp.zeros_like(out)
    out[0 : left.shape[0], 0 : left.shape[1]] = left[...]
    out[3 : 3 + right.shape[0], 0 : right.shape[1]] = right[...]


def right_products(right, slots, begin, end, rows, lowest, inter, env, total):
    def chunks(at, unroll):
        done = []
        for step in range(unroll):
            base = at + step * DEPTH
            first = [inter[right[base + i], rows, :] for i in range(DEPTH)]
            second = [env[right[slots + base + i]] for i in range(DEPTH)]
            product = jnp.dot(
                jnp.concatenate(first, axis=1),
                jnp.concatenate(second, axis=0),
                preferred_element_type=jnp.float32,
            )
            place = jnp.minimum(right[2 * slots + base] - lowest, total.shape[0] - 1)
            done.append((place, product))
        for place, product in done:
            total[place] += product

    turn = RIGHT_UNROLL * DEPTH
    for width in (4, 2, 1):
        rounds = (end - begin) // width

        @pl.loop(0, rounds)
        def _(step, begin=begin, width=width):
            chunks((begin + step * width) * turn, width * RIGHT_UNROLL)

        begin = begin + rounds * width


def turn_of(right, slots, which):
    turn = RIGHT_UNROLL * DEPTH
    return lax.div(right[3 * slots + which] + turn - 1, turn)


def part_rows(part, share):
    return pl.ds(pl.multiple_of(part * share, share), share)


def join(near, pieces, row, out, sems):
    copies = []
    for place, piece in enumerate(pieces):
        span = pl.ds(place * piece.shape[0], piece.shape[0])
        if near:
            out[span] = piece[:, row]
        else:
            copies.append(pltpu.make_async_copy(piece.at[:, row], out.at[span], sems.at[place]))
    for copy in copies:
        copy.start()
    for copy in copies:
        copy.wait()


def first_kernel(
    count,
    slots,
    near,
    listed_left,
    listed_right,
    wave,
    here_left,
    there_left,
    here_right,
    there_right,
    inter,
    send,
    env_right,
    env_left,
    acc,
    total,
    left,
    right,
    sems,
):
    lists = [
        pltpu.make_async_copy(listed_left, left, sems.at[2]),
        pltpu.make_async_copy(listed_right, right, sems.at[3]),
    ]
    for copy in lists:
        copy.start()
    inters, rows, dim = acc.shape
    acc[...] = jnp.zeros_like(acc)
    total[...] = jnp.zeros_like(total)
    inter[inters] = jnp.zeros((rows, dim), jnp.bfloat16)
    parts, share = send.shape[0] + 1, total.shape[1]
    term = lax.axis_index("term")
    vector = lax.rem(term, parts)
    first_row = 0 if rows == dim else pl.multiple_of(lax.div(term, parts) * rows, rows)
    join(near, (here_left, there_left), pl.ds(first_row, rows), env_left, sems)
    join(near, (here_right, there_right), pl.ds(0, dim), env_right, sems)
    for copy in lists:
        copy.wait()

    @pl.loop(0, count // LEFT_UNROLL)
    def _(turn):
        done = []
        for step in range(LEFT_UNROLL):
            at = turn * LEFT_UNROLL + step
            product = jnp.dot(
                env_left[left[at]], wave[left[count + at]], preferred_element_type=jnp.float32
            )
            done.append((left[2 * count + at], product))
        for place, product in done:
            acc[place] += product

    @pl.loop(0, inters // 8)
    def _(turn):
        for step in range(8):
            inter[turn * 8 + step] = acc[turn * 8 + step].astype(jnp.bfloat16)

    for hop in range(1, parts):
        if hop > 1:
            total[...] = jnp.zeros_like(total)
        own = part_rows(lax.rem(vector + hop, parts), share)
        right_products(right, slots, 0, turn_of(right, slots, 0), own, 0, inter, env_right, total)
        send[hop - 1] = total[...].astype(jnp.bfloat16)


def both_kernel(slots, cut, listed, inter, env, send, keep, total, right, sem):
    lists = pltpu.make_async_copy(listed, right, sem)
    lists.start()
    total[...] = jnp.zeros_like(total)
    lists.wait()
    parts, share = send.shape[0] + 1, keep.shape[1]
    vector = lax.rem(lax.axis_index("term"), parts)
    begin, end = turn_of(right, slots, 0), turn_of(right, slots, 1)
    right_products(right, slots, begin, end, pl.ds(0, total.shape[1]), cut, inter, env, total)
    for hop in range(1, parts):
        rows = part_rows(lax.rem(vector + hop, parts), share)
        send[hop - 1] = total[:, rows, :].astype(jnp.bfloat16)
    keep[...] = total[:, part_rows(vector, share), :]


def own_kernel(slots, parts, listed, inter, env, keep, right, sem):
    lists = pltpu.make_async_copy(listed, right, sem)
    lists.start()
    keep[...] = jnp.zeros_like(keep)
    lists.wait()
    rows = part_rows(lax.rem(lax.axis_index("term"), parts), keep.shape[1])
    right_products(right, slots, 0, turn_of(right, slots, 0), rows, 0, inter, env, keep)


def finish_kernel(vectors, *refs):
    pieces, (out, held, sems) = refs[: 2 * vectors], refs[2 * vectors :]
    vector = lax.rem(lax.axis_index("term"), vectors)
    copies = []
    for hop in range(vectors):
        place = lax.rem(vector + vectors - hop, vectors)
        first = 0
        for part in range(2):
            source = pieces[2 * hop + part]
            span = pl.ds(first, source.shape[0])
            if hop > 0:
                held[hop - 1, span] = source[...].astype(jnp.float32)
                source = held.at[hop - 1, span]
            copies.append(
                pltpu.make_async_copy(source, out.at[span, place], sems.at[2 * hop + part])
            )
            copies[-1].start()
            first += span.size
    for copy in copies:
        copy.wait()


def shards(wave_tiles, left_env, right_env, send_list, left_tasks, right_tasks):
    sectors, terms = lax.axis_size("sector"), lax.axis_size("term")
    tiles, vectors, dim, _ = wave_tiles.shape
    term = lax.axis_index("term")
    blocks = terms // vectors
    rows, share = dim // blocks, dim // terms
    vector, block = term % vectors, term // vectors

    vmem = pl.BlockSpec(memory_space=pltpu.VMEM)
    hbm = pl.BlockSpec(memory_space=pl.ANY)
    send_slots = send_list.shape[1]
    tile_bytes = dim * dim * 2
    outgoing, env = pl.pallas_call(
        functools.partial(pack_kernel, vectors),
        out_shape=(
            jax.ShapeDtypeStruct((send_slots, dim, dim), jnp.bfloat16),
            jax.ShapeDtypeStruct((2, dim, dim), jnp.bfloat16),
        ),
        in_specs=[hbm, hbm, hbm, hbm],
        out_specs=(vmem, vmem),
        scratch_shapes=[
            pltpu.VMEM((tiles, dim, dim), jnp.bfloat16),
            pltpu.SMEM(send_list.shape, jnp.int32),
            pltpu.SemaphoreType.DMA((4,)),
        ],
        compiler_params=vmem_params(54 << 20),
        name="pack",
    )(send_list, wave_tiles, left_env, right_env)
    column = gather_far(env)
    received = lax.all_to_all(outgoing, "sector", split_axis=0, concat_axis=0, tiled=True)
    sides = gather_env(column)

    left_count, right_count = left_tasks.shape[2], right_tasks.shape[2]
    tasks = pl.pallas_call(
        tasks_kernel,
        out_shape=jax.ShapeDtypeStruct((8, max(left_count, right_count)), jnp.int32),
        in_specs=[vmem, vmem, hbm],
        out_specs=vmem,
        compiler_params=vmem_params(0),
        name="tasks",
    )(left_tasks[0, 0].T, right_tasks[0, 0].T, column[0])[None]
    bit = 1
    while bit < terms:
        tasks = jnp.concatenate([tasks, swap(tasks, "term", bit)], axis=0)
        bit *= 2

    def listed(first_row, count):
        rows = jnp.swapaxes(tasks[:, first_row : first_row + 3, :count], 0, 1).reshape(3, -1)
        group = (jnp.arange(terms * count, dtype=jnp.int32) // count) ^ term
        return rows[0], rows[1], rows[2], group

    left_env_tile, left_slot, left_inter, left_group = listed(0, left_count)
    right_inter, right_env_tile, right_sigma, right_group = listed(3, right_count)
    left_count, right_count = terms * left_count, terms * right_count
    left = jnp.concatenate(
        [
            env_place(left_group, left_env_tile),
            left_slot,
            left_group * INTER_TILES + left_inter,
        ]
    )
    turn = DEPTH * RIGHT_UNROLL
    slots = round_up(right_count + tiles * (DEPTH - 1), turn) + turn
    cut = tiles * 11 // 16
    inters = terms * INTER_TILES
    right = schedule(
        right_group * INTER_TILES + right_inter,
        env_place(right_group, right_env_tile),
        right_sigma,
        tiles,
        cut,
        DEPTH,
        turn,
        slots,
        inters,
    )
    block_bytes = rows * dim * 2
    env_tiles = terms * sectors
    env_bytes = env_tiles * tile_bytes
    near = env_bytes <= 2 << 20
    env_spec = vmem if near else hbm
    right_bytes = (tiles * 2 + inters) * block_bytes + env_bytes
    first_bytes = right_bytes + send_slots * tile_bytes + (2 * inters + env_tiles) * block_bytes
    right_params = vmem_params(right_bytes)

    def sent(count):
        return jax.ShapeDtypeStruct((vectors - 1, count, share, dim), jnp.bfloat16)

    def cost(part):
        flops = 2 * right_count * rows * dim * dim // part
        return pl.CostEstimate(flops=flops, bytes_accessed=12 << 20, transcendentals=0)

    inter, send_one, env_right = pl.pallas_call(
        functools.partial(first_kernel, left_count, slots, near),
        out_shape=(
            jax.ShapeDtypeStruct((inters + 1, rows, dim), jnp.bfloat16),
            sent(cut),
            jax.ShapeDtypeStruct((env_tiles, dim, dim), jnp.bfloat16),
        ),
        in_specs=[hbm, hbm, vmem] + [env_spec] * 4,
        out_specs=(vmem, vmem, vmem),
        scratch_shapes=[
            pltpu.VMEM((env_tiles, rows, dim), jnp.bfloat16),
            pltpu.VMEM((inters, rows, dim), jnp.float32),
            pltpu.VMEM((cut, share, dim), jnp.float32),
            pltpu.SMEM(left.shape, jnp.int32),
            pltpu.SMEM(right.shape, jnp.int32),
            pltpu.SemaphoreType.DMA((4,)),
        ],
        compiler_params=vmem_params(first_bytes + near * 2 * env_bytes),
        name="first_products",
    )(left, right, received, *sides[0], *sides[1])
    send_two, keep_two = pl.pallas_call(
        functools.partial(both_kernel, slots, cut),
        out_shape=(
            sent(tiles - cut),
            jax.ShapeDtypeStruct((tiles - cut, share, dim), jnp.float32),
        ),
        in_specs=[hbm, vmem, vmem],
        out_specs=(vmem, vmem),
        scratch_shapes=[
            pltpu.VMEM((tiles - cut, rows, dim), jnp.float32),
            pltpu.SMEM(right.shape, jnp.int32),
            pltpu.SemaphoreType.DMA,
        ],
        compiler_params=right_params,
        cost_estimate=cost(2),
        name="both_products",
    )(right, inter, env_right)
    keep_one = pl.pallas_call(
        functools.partial(own_kernel, slots, vectors),
        out_shape=jax.ShapeDtypeStruct((cut, share, dim), jnp.float32),
        in_specs=[hbm, vmem, vmem],
        out_specs=vmem,
        scratch_shapes=[pltpu.SMEM(right.shape, jnp.int32), pltpu.SemaphoreType.DMA],
        compiler_params=right_params,
        cost_estimate=cost(vectors),
        name="own_products",
    )(right, inter, env_right)
    pieces = [keep_one, keep_two]
    for hop in range(1, vectors):
        pairs = [
            (i, i // vectors * vectors + (i % vectors + hop) % vectors) for i in range(terms)
        ]
        pieces += [lax.ppermute(send[hop - 1], "term", pairs) for send in (send_one, send_two)]
    return pl.pallas_call(
        functools.partial(finish_kernel, vectors),
        out_shape=jax.ShapeDtypeStruct((tiles, vectors, share, dim), jnp.float32),
        in_specs=[vmem] * (2 * vectors),
        out_specs=hbm,
        scratch_shapes=[
            pltpu.VMEM((vectors - 1, tiles, share, dim), jnp.float32),
            pltpu.SemaphoreType.DMA((2 * vectors,)),
        ],
        compiler_params=vmem_params(3 * vectors * tiles * share * dim * 4),
        name="finish",
    )(*pieces)


def solution(mesh):
    in_specs = (
        P("sector", None, None, None),
        P("term", "sector", None, None),
        P("term", "sector", None, None),
        P("sector", None),
        P("term", "sector", None, None),
        P("term", "sector", None, None),
    )
    out_specs = P("sector", None, "term", None)
    return jax.shard_map(shards, mesh=mesh, in_specs=in_specs, out_specs=out_specs, check_vma=False)
```

```python
import functools

import jax
import jax.numpy as jnp
from jax import lax
from jax.experimental import pallas as pl
from jax.experimental.pallas import tpu as pltpu
from jax.sharding import PartitionSpec as P

INTER_TILES = 32
PACK_UNROLL = 8
DEPTH = 8
LEFT_UNROLL = 96
RIGHT_UNROLL = 4


def vmem_params(size):
    return pltpu.CompilerParams(vmem_limit_bytes=min(size + (6 << 20), 60 << 20))


def round_up(value, step):
    return -(-value // step) * step


def swap(value, axis, mask):
    size = lax.axis_size(axis)
    return lax.ppermute(value, axis, [(i, i ^ mask) for i in range(size)])


def cross(value, first):
    sectors, terms = lax.axis_size("sector"), lax.axis_size("term")
    pairs = []
    for i in range(terms * sectors):
        pairs.append((i, i ^ (sectors if (i & 1) == first else 2)))
    return lax.ppermute(value, ("term", "sector"), pairs)


def env_place(group, tile):
    sectors, terms = lax.axis_size("sector"), lax.axis_size("term")
    core = tile & 1
    group = group ^ lax.axis_index("term")
    tile = tile ^ lax.axis_index("sector")
    far = sectors // 4
    over, across = group & 1, (tile >> 1) & 1
    square = jnp.where(core == 0, over + 2 * across, across + 2 * over)
    place = (tile >> 2) + far * (square + 4 * (group >> 1))
    return place + far * 2 * terms * (tile & 1)


def column_kernel(count, *refs):
    tiles, sides = refs[:count], refs[count:]
    for place in range(count):
        for side in range(2):
            sides[side][place] = tiles[place][side]


def gather_far(env):
    count = lax.axis_size("sector") // 4
    vmem = pl.BlockSpec(memory_space=pltpu.VMEM)
    return pl.pallas_call(
        functools.partial(column_kernel, count),
        out_shape=[jax.ShapeDtypeStruct((count,) + env.shape[1:], env.dtype)] * 2,
        in_specs=[vmem] * count,
        out_specs=[vmem] * 2,
        compiler_params=vmem_params(4 * count * env.size),
        name="column",
    )(env, *[swap(env, "sector", mask << 2) for mask in range(1, count)])


def gather_env(column):
    terms = lax.axis_size("term")
    sides = []
    for side in range(2):
        one, two = cross(column[side], 0), cross(column[side], 1)
        plane = jnp.concatenate([column[side], one, two, cross(one, 1)])
        bit = 2
        while bit < terms:
            plane = jnp.concatenate([plane, swap(plane, "term", bit)])
            bit *= 2
        sides.append((plane, swap(plane, "sector", 1)))
    return sides


def pack_kernel(vectors, listed, wave, left, right, out, env, held, picks, sems):
    vector = lax.rem(lax.axis_index("term"), vectors)
    copies = [
        pltpu.make_async_copy(wave.at[:, vector], held, sems.at[0]),
        pltpu.make_async_copy(left.at[0, 0], env.at[0], sems.at[1]),
        pltpu.make_async_copy(right.at[0, 0], env.at[1], sems.at[2]),
        pltpu.make_async_copy(listed, picks, sems.at[3]),
    ]
    for copy in copies:
        copy.start()
    copies[0].wait()
    copies[3].wait()

    @pl.loop(0, out.shape[0] // PACK_UNROLL)
    def _(turn):
        for step in range(PACK_UNROLL):
            slot = turn * PACK_UNROLL + step
            tile = picks[0, slot]
            picked = held[jnp.maximum(tile, 0)]
            out[slot] = jnp.where(tile >= 0, picked, jnp.zeros_like(picked))

    copies[1].wait()
    copies[2].wait()


def schedule(first, second, target, targets, cut, depth, turn, slots, idle):
    count = target.shape[0]
    index = jnp.arange(count, dtype=jnp.int32)
    same = target[:, None] == target[None, :]
    rank = jnp.sum(same & (index[None, :] < index[:, None]), axis=1, dtype=jnp.int32)
    names = jnp.arange(targets, dtype=jnp.int32)
    counts = jnp.sum(target[None, :] == names[:, None], axis=1, dtype=jnp.int32)
    padded = (counts + depth - 1) // depth * depth

    def before(bounds):
        lower = names[None, :] < bounds[:, None]
        return jnp.sum(jnp.where(lower, padded[None, :], 0), axis=1, dtype=jnp.int32)

    head = before(jnp.full((targets,), cut, jnp.int32))
    padded = padded + jnp.where(names == cut - 1, -head & (turn - 1), 0)
    starts = before(target)
    place = starts + rank
    chosen = place[None, :] == jnp.arange(slots, dtype=jnp.int32)[:, None]

    def pick(values, rest):
        return rest + jnp.sum(jnp.where(chosen, values[None, :] - rest, 0), axis=1, dtype=jnp.int32)

    ends = before(cut + (targets - cut) * jnp.arange(2, dtype=jnp.int32))
    return jnp.concatenate([pick(first, idle), pick(second, 0), pick(target, cut), ends])


def tasks_kernel(left, right, after, out):
    out[...] = jnp.zeros_like(out)
    out[0 : left.shape[0], 0 : left.shape[1]] = left[...]
    out[3 : 3 + right.shape[0], 0 : right.shape[1]] = right[...]


def right_products(right, slots, begin, end, rows, lowest, inter, env, total):
    def chunks(at, unroll):
        done = []
        for step in range(unroll):
            base = at + step * DEPTH
            first = [inter[right[base + i], rows, :] for i in range(DEPTH)]
            second = [env[right[slots + base + i]] for i in range(DEPTH)]
            product = jnp.dot(
                jnp.concatenate(first, axis=1),
                jnp.concatenate(second, axis=0),
                preferred_element_type=jnp.float32,
            )
            place = jnp.minimum(right[2 * slots + base] - lowest, total.shape[0] - 1)
            done.append((place, product))
        for place, product in done:
            total[place] += product

    turn = RIGHT_UNROLL * DEPTH
    for width in (4, 2, 1):
        rounds = (end - begin) // width

        @pl.loop(0, rounds)
        def _(step, begin=begin, width=width):
            chunks((begin + step * width) * turn, width * RIGHT_UNROLL)

        begin = begin + rounds * width


def turn_of(right, slots, which):
    turn = RIGHT_UNROLL * DEPTH
    return lax.div(right[3 * slots + which] + turn - 1, turn)


def part_rows(part, share):
    return pl.ds(pl.multiple_of(part * share, share), share)


def join(near, pieces, row, out, sems):
    copies = []
    for place, piece in enumerate(pieces):
        span = pl.ds(place * piece.shape[0], piece.shape[0])
        if near:
            out[span] = piece[:, row]
        else:
            copies.append(pltpu.make_async_copy(piece.at[:, row], out.at[span], sems.at[place]))
    for copy in copies:
        copy.start()
    for copy in copies:
        copy.wait()


def first_kernel(
    count,
    slots,
    near,
    listed_left,
    listed_right,
    wave,
    here_left,
    there_left,
    here_right,
    there_right,
    inter,
    send,
    env_right,
    env_left,
    acc,
    total,
    left,
    right,
    sems,
):
    lists = [
        pltpu.make_async_copy(listed_left, left, sems.at[2]),
        pltpu.make_async_copy(listed_right, right, sems.at[3]),
    ]
    for copy in lists:
        copy.start()
    inters, rows, dim = acc.shape
    acc[...] = jnp.zeros_like(acc)
    total[...] = jnp.zeros_like(total)
    inter[inters] = jnp.zeros((rows, dim), jnp.bfloat16)
    parts, share = send.shape[0] + 1, total.shape[1]
    term = lax.axis_index("term")
    vector = lax.rem(term, parts)
    first_row = 0 if rows == dim else pl.multiple_of(lax.div(term, parts) * rows, rows)
    join(near, (here_left, there_left), pl.ds(first_row, rows), env_left, sems)
    join(near, (here_right, there_right), pl.ds(0, dim), env_right, sems)
    lists[0].wait()

    @pl.loop(0, count // LEFT_UNROLL)
    def _(turn):
        done = []
        for step in range(LEFT_UNROLL):
            at = turn * LEFT_UNROLL + step
            product = jnp.dot(
                env_left[left[at]], wave[left[count + at]], preferred_element_type=jnp.float32
            )
            done.append((left[2 * count + at], product))
        for place, product in done:
            acc[place] += product

    @pl.loop(0, inters // 8)
    def _(turn):
        for step in range(8):
            inter[turn * 8 + step] = acc[turn * 8 + step].astype(jnp.bfloat16)

    lists[1].wait()
    for hop in range(1, parts):
        if hop > 1:
            total[...] = jnp.zeros_like(total)
        own = part_rows(lax.rem(vector + hop, parts), share)
        right_products(right, slots, 0, turn_of(right, slots, 0), own, 0, inter, env_right, total)
        send[hop - 1] = total[...].astype(jnp.bfloat16)


def both_kernel(slots, cut, listed, inter, env, send, keep, total, right, sem):
    lists = pltpu.make_async_copy(listed, right, sem)
    lists.start()
    total[...] = jnp.zeros_like(total)
    lists.wait()
    parts, share = send.shape[0] + 1, keep.shape[1]
    vector = lax.rem(lax.axis_index("term"), parts)
    begin, end = turn_of(right, slots, 0), turn_of(right, slots, 1)
    right_products(right, slots, begin, end, pl.ds(0, total.shape[1]), cut, inter, env, total)
    for hop in range(1, parts):
        rows = part_rows(lax.rem(vector + hop, parts), share)
        send[hop - 1] = total[:, rows, :].astype(jnp.bfloat16)
    keep[...] = total[:, part_rows(vector, share), :]


def own_kernel(slots, parts, listed, inter, env, keep, right, sem):
    lists = pltpu.make_async_copy(listed, right, sem)
    lists.start()
    keep[...] = jnp.zeros_like(keep)
    lists.wait()
    rows = part_rows(lax.rem(lax.axis_index("term"), parts), keep.shape[1])
    right_products(right, slots, 0, turn_of(right, slots, 0), rows, 0, inter, env, keep)


def finish_kernel(vectors, *refs):
    pieces, (out, held, sems) = refs[: 2 * vectors], refs[2 * vectors :]
    vector = lax.rem(lax.axis_index("term"), vectors)
    copies = []
    for hop in range(vectors):
        place = lax.rem(vector + vectors - hop, vectors)
        first = 0
        for part in range(2):
            source = pieces[2 * hop + part]
            span = pl.ds(first, source.shape[0])
            if hop > 0:
                held[hop - 1, span] = source[...].astype(jnp.float32)
                source = held.at[hop - 1, span]
            copies.append(
                pltpu.make_async_copy(source, out.at[span, place], sems.at[2 * hop + part])
            )
            copies[-1].start()
            first += span.size
    for copy in copies:
        copy.wait()


def shards(wave_tiles, left_env, right_env, send_list, left_tasks, right_tasks):
    sectors, terms = lax.axis_size("sector"), lax.axis_size("term")
    tiles, vectors, dim, _ = wave_tiles.shape
    term = lax.axis_index("term")
    blocks = terms // vectors
    rows, share = dim // blocks, dim // terms
    vector, block = term % vectors, term // vectors

    vmem = pl.BlockSpec(memory_space=pltpu.VMEM)
    hbm = pl.BlockSpec(memory_space=pl.ANY)
    send_slots = send_list.shape[1]
    tile_bytes = dim * dim * 2
    outgoing, env = pl.pallas_call(
        functools.partial(pack_kernel, vectors),
        out_shape=(
            jax.ShapeDtypeStruct((send_slots, dim, dim), jnp.bfloat16),
            jax.ShapeDtypeStruct((2, dim, dim), jnp.bfloat16),
        ),
        in_specs=[hbm, hbm, hbm, hbm],
        out_specs=(vmem, vmem),
        scratch_shapes=[
            pltpu.VMEM((tiles, dim, dim), jnp.bfloat16),
            pltpu.SMEM(send_list.shape, jnp.int32),
            pltpu.SemaphoreType.DMA((4,)),
        ],
        compiler_params=vmem_params(54 << 20),
        name="pack",
    )(send_list, wave_tiles, left_env, right_env)
    column = gather_far(env)
    received = lax.all_to_all(outgoing, "sector", split_axis=0, concat_axis=0, tiled=True)
    sides = gather_env(column)

    left_count, right_count = left_tasks.shape[2], right_tasks.shape[2]
    tasks = pl.pallas_call(
        tasks_kernel,
        out_shape=jax.ShapeDtypeStruct((8, max(left_count, right_count)), jnp.int32),
        in_specs=[vmem, vmem, hbm],
        out_specs=vmem,
        compiler_params=vmem_params(0),
        name="tasks",
    )(left_tasks[0, 0].T, right_tasks[0, 0].T, column[0])[None]
    bit = 1
    while bit < terms:
        tasks = jnp.concatenate([tasks, swap(tasks, "term", bit)], axis=0)
        bit *= 2

    def listed(first_row, count):
        rows = jnp.swapaxes(tasks[:, first_row : first_row + 3, :count], 0, 1).reshape(3, -1)
        group = (jnp.arange(terms * count, dtype=jnp.int32) // count) ^ term
        return rows[0], rows[1], rows[2], group

    left_env_tile, left_slot, left_inter, left_group = listed(0, left_count)
    right_inter, right_env_tile, right_sigma, right_group = listed(3, right_count)
    left_count, right_count = terms * left_count, terms * right_count
    left = jnp.concatenate(
        [
            env_place(left_group, left_env_tile),
            left_slot,
            left_group * INTER_TILES + left_inter,
        ]
    )
    turn = DEPTH * RIGHT_UNROLL
    slots = round_up(right_count + tiles * (DEPTH - 1), turn) + turn
    cut = tiles * 11 // 16
    inters = terms * INTER_TILES
    right = schedule(
        right_group * INTER_TILES + right_inter,
        env_place(right_group, right_env_tile),
        right_sigma,
        tiles,
        cut,
        DEPTH,
        turn,
        slots,
        inters,
    )
    block_bytes = rows * dim * 2
    env_tiles = terms * sectors
    env_bytes = env_tiles * tile_bytes
    near = env_bytes <= 2 << 20
    env_spec = vmem if near else hbm
    right_bytes = (tiles * 2 + inters) * block_bytes + env_bytes
    first_bytes = right_bytes + send_slots * tile_bytes + (2 * inters + env_tiles) * block_bytes
    right_params = vmem_params(right_bytes)

    def sent(count):
        return jax.ShapeDtypeStruct((vectors - 1, count, share, dim), jnp.bfloat16)

    def cost(part):
        flops = 2 * right_count * rows * dim * dim // part
        return pl.CostEstimate(flops=flops, bytes_accessed=12 << 20, transcendentals=0)

    inter, send_one, env_right = pl.pallas_call(
        functools.partial(first_kernel, left_count, slots, near),
        out_shape=(
            jax.ShapeDtypeStruct((inters + 1, rows, dim), jnp.bfloat16),
            sent(cut),
            jax.ShapeDtypeStruct((env_tiles, dim, dim), jnp.bfloat16),
        ),
        in_specs=[hbm, hbm, vmem] + [env_spec] * 4,
        out_specs=(vmem, vmem, vmem),
        scratch_shapes=[
            pltpu.VMEM((env_tiles, rows, dim), jnp.bfloat16),
            pltpu.VMEM((inters, rows, dim), jnp.float32),
            pltpu.VMEM((cut, share, dim), jnp.float32),
            pltpu.SMEM(left.shape, jnp.int32),
            pltpu.SMEM(right.shape, jnp.int32),
            pltpu.SemaphoreType.DMA((4,)),
        ],
        compiler_params=vmem_params(first_bytes + near * 2 * env_bytes),
        name="first_products",
    )(left, right, received, *sides[0], *sides[1])
    send_two, keep_two = pl.pallas_call(
        functools.partial(both_kernel, slots, cut),
        out_shape=(
            sent(tiles - cut),
            jax.ShapeDtypeStruct((tiles - cut, share, dim), jnp.float32),
        ),
        in_specs=[hbm, vmem, vmem],
        out_specs=(vmem, vmem),
        scratch_shapes=[
            pltpu.VMEM((tiles - cut, rows, dim), jnp.float32),
            pltpu.SMEM(right.shape, jnp.int32),
            pltpu.SemaphoreType.DMA,
        ],
        compiler_params=right_params,
        cost_estimate=cost(2),
        name="both_products",
    )(right, inter, env_right)
    keep_one = pl.pallas_call(
        functools.partial(own_kernel, slots, vectors),
        out_shape=jax.ShapeDtypeStruct((cut, share, dim), jnp.float32),
        in_specs=[hbm, vmem, vmem],
        out_specs=vmem,
        scratch_shapes=[pltpu.SMEM(right.shape, jnp.int32), pltpu.SemaphoreType.DMA],
        compiler_params=right_params,
        cost_estimate=cost(vectors),
        name="own_products",
    )(right, inter, env_right)
    pieces = [keep_one, keep_two]
    for hop in range(1, vectors):
        pairs = [
            (i, i // vectors * vectors + (i % vectors + hop) % vectors) for i in range(terms)
        ]
        pieces += [lax.ppermute(send[hop - 1], "term", pairs) for send in (send_one, send_two)]
    return pl.pallas_call(
        functools.partial(finish_kernel, vectors),
        out_shape=jax.ShapeDtypeStruct((tiles, vectors, share, dim), jnp.float32),
        in_specs=[vmem] * (2 * vectors),
        out_specs=hbm,
        scratch_shapes=[
            pltpu.VMEM((vectors - 1, tiles, share, dim), jnp.float32),
            pltpu.SemaphoreType.DMA((2 * vectors,)),
        ],
        compiler_params=vmem_params(3 * vectors * tiles * share * dim * 4),
        name="finish",
    )(*pieces)


def solution(mesh):
    in_specs = (
        P("sector", None, None, None),
        P("term", "sector", None, None),
        P("term", "sector", None, None),
        P("sector", None),
        P("term", "sector", None, None),
        P("term", "sector", None, None),
    )
    out_specs = P("sector", None, "term", None)
    return jax.shard_map(shards, mesh=mesh, in_specs=in_specs, out_specs=out_specs, check_vma=False)
```

```python
import functools

import jax
import jax.numpy as jnp
from jax import lax
from jax.experimental import pallas as pl
from jax.experimental.pallas import tpu as pltpu
from jax.sharding import PartitionSpec as P

INTER_TILES = 32
PACK_UNROLL = 8
DEPTH = 8
LEFT_UNROLL = 96
RIGHT_UNROLL = 4


def vmem_params(size):
    return pltpu.CompilerParams(vmem_limit_bytes=min(size + (6 << 20), 60 << 20))


def round_up(value, step):
    return -(-value // step) * step


def swap(value, axis, mask):
    size = lax.axis_size(axis)
    return lax.ppermute(value, axis, [(i, i ^ mask) for i in range(size)])


def cross(value, first):
    sectors, terms = lax.axis_size("sector"), lax.axis_size("term")
    pairs = []
    for i in range(terms * sectors):
        pairs.append((i, i ^ (sectors if (i & 1) == first else 2)))
    return lax.ppermute(value, ("term", "sector"), pairs)


def env_place(group, tile):
    sectors, terms = lax.axis_size("sector"), lax.axis_size("term")
    core = tile & 1
    group = group ^ lax.axis_index("term")
    tile = tile ^ lax.axis_index("sector")
    far = sectors // 4
    over, across = group & 1, (tile >> 1) & 1
    square = jnp.where(core == 0, over + 2 * across, across + 2 * over)
    place = (tile >> 2) + far * (square + 4 * (group >> 1))
    return place + far * 2 * terms * (tile & 1)


def column_kernel(count, *refs):
    tiles, sides = refs[:count], refs[count:]
    for place in range(count):
        for side in range(2):
            sides[side][place] = tiles[place][side]


def gather_far(env):
    count = lax.axis_size("sector") // 4
    vmem = pl.BlockSpec(memory_space=pltpu.VMEM)
    return pl.pallas_call(
        functools.partial(column_kernel, count),
        out_shape=[jax.ShapeDtypeStruct((count,) + env.shape[1:], env.dtype)] * 2,
        in_specs=[vmem] * count,
        out_specs=[vmem] * 2,
        compiler_params=vmem_params(4 * count * env.size),
        name="column",
    )(env, *[swap(env, "sector", mask << 2) for mask in range(1, count)])


def gather_env(column):
    terms = lax.axis_size("term")
    sides = []
    for side in range(2):
        one, two = cross(column[side], 0), cross(column[side], 1)
        plane = jnp.concatenate([column[side], one, two, cross(one, 1)])
        bit = 2
        while bit < terms:
            plane = jnp.concatenate([plane, swap(plane, "term", bit)])
            bit *= 2
        sides.append((plane, swap(plane, "sector", 1)))
    return sides


def pack_kernel(vectors, listed, wave, left, right, out, env, held, picks, sems):
    vector = lax.rem(lax.axis_index("term"), vectors)
    copies = [
        pltpu.make_async_copy(wave.at[:, vector], held, sems.at[0]),
        pltpu.make_async_copy(left.at[0, 0], env.at[0], sems.at[1]),
        pltpu.make_async_copy(right.at[0, 0], env.at[1], sems.at[2]),
        pltpu.make_async_copy(listed, picks, sems.at[3]),
    ]
    for copy in copies:
        copy.start()
    copies[0].wait()
    copies[3].wait()

    @pl.loop(0, out.shape[0] // PACK_UNROLL)
    def _(turn):
        for step in range(PACK_UNROLL):
            slot = turn * PACK_UNROLL + step
            tile = picks[0, slot]
            picked = held[jnp.maximum(tile, 0)]
            out[slot] = jnp.where(tile >= 0, picked, jnp.zeros_like(picked))

    copies[1].wait()
    copies[2].wait()


def schedule(first, second, target, targets, cut, depth, turn, slots, idle):
    count = target.shape[0]
    index = jnp.arange(count, dtype=jnp.int32)
    same = target[:, None] == target[None, :]
    rank = jnp.sum(same & (index[None, :] < index[:, None]), axis=1, dtype=jnp.int32)
    names = jnp.arange(targets, dtype=jnp.int32)
    counts = jnp.sum(target[None, :] == names[:, None], axis=1, dtype=jnp.int32)
    padded = (counts + depth - 1) // depth * depth

    def before(bounds):
        lower = names[None, :] < bounds[:, None]
        return jnp.sum(jnp.where(lower, padded[None, :], 0), axis=1, dtype=jnp.int32)

    head = before(jnp.full((targets,), cut, jnp.int32))
    padded = padded + jnp.where(names == cut - 1, -head & (turn - 1), 0)
    starts = before(target)
    place = starts + rank
    chosen = place[None, :] == jnp.arange(slots, dtype=jnp.int32)[:, None]

    def pick(values, rest):
        return rest + jnp.sum(jnp.where(chosen, values[None, :] - rest, 0), axis=1, dtype=jnp.int32)

    ends = before(cut + (targets - cut) * jnp.arange(2, dtype=jnp.int32))
    return jnp.concatenate([pick(first, idle), pick(second, 0), pick(target, cut), ends])


def tasks_kernel(left, right, after, out):
    out[...] = jnp.zeros_like(out)
    out[0 : left.shape[0], 0 : left.shape[1]] = left[...]
    out[3 : 3 + right.shape[0], 0 : right.shape[1]] = right[...]


def right_products(right, slots, begin, end, rows, lowest, inter, env, total):
    def chunks(at, unroll):
        done = []
        for step in range(unroll):
            base = at + step * DEPTH
            first = [inter[right[base + i], rows, :] for i in range(DEPTH)]
            second = [env[right[slots + base + i]] for i in range(DEPTH)]
            product = jnp.dot(
                jnp.concatenate(first, axis=1),
                jnp.concatenate(second, axis=0),
                preferred_element_type=jnp.float32,
            )
            place = jnp.minimum(right[2 * slots + base] - lowest, total.shape[0] - 1)
            done.append((place, product))
        for place, product in done:
            total[place] += product

    turn = RIGHT_UNROLL * DEPTH
    for width in (8, 4, 2, 1):
        rounds = (end - begin) // width

        @pl.loop(0, rounds)
        def _(step, begin=begin, width=width):
            chunks((begin + step * width) * turn, width * RIGHT_UNROLL)

        begin = begin + rounds * width


def turn_of(right, slots, which):
    turn = RIGHT_UNROLL * DEPTH
    return lax.div(right[3 * slots + which] + turn - 1, turn)


def part_rows(part, share):
    return pl.ds(pl.multiple_of(part * share, share), share)


def join(near, pieces, row, out, sems):
    copies = []
    for place, piece in enumerate(pieces):
        span = pl.ds(place * piece.shape[0], piece.shape[0])
        if near:
            out[span] = piece[:, row]
        else:
            copies.append(pltpu.make_async_copy(piece.at[:, row], out.at[span], sems.at[place]))
    for copy in copies:
        copy.start()
    for copy in copies:
        copy.wait()


def first_kernel(
    count,
    slots,
    near,
    listed_left,
    listed_right,
    wave,
    here_left,
    there_left,
    here_right,
    there_right,
    inter,
    send,
    env_right,
    env_left,
    acc,
    total,
    left,
    right,
    sems,
):
    lists = [
        pltpu.make_async_copy(listed_left, left, sems.at[2]),
        pltpu.make_async_copy(listed_right, right, sems.at[3]),
    ]
    for copy in lists:
        copy.start()
    inters, rows, dim = acc.shape
    acc[...] = jnp.zeros_like(acc)
    total[...] = jnp.zeros_like(total)
    inter[inters] = jnp.zeros((rows, dim), jnp.bfloat16)
    parts, share = send.shape[0] + 1, total.shape[1]
    term = lax.axis_index("term")
    vector = lax.rem(term, parts)
    first_row = 0 if rows == dim else pl.multiple_of(lax.div(term, parts) * rows, rows)
    join(near, (here_left, there_left), pl.ds(first_row, rows), env_left, sems)
    join(near, (here_right, there_right), pl.ds(0, dim), env_right, sems)
    lists[0].wait()

    @pl.loop(0, count // LEFT_UNROLL)
    def _(turn):
        done = []
        for step in range(LEFT_UNROLL):
            at = turn * LEFT_UNROLL + step
            product = jnp.dot(
                env_left[left[at]], wave[left[count + at]], preferred_element_type=jnp.float32
            )
            done.append((left[2 * count + at], product))
        for place, product in done:
            acc[place] += product

    @pl.loop(0, inters // 8)
    def _(turn):
        for step in range(8):
            inter[turn * 8 + step] = acc[turn * 8 + step].astype(jnp.bfloat16)

    lists[1].wait()
    for hop in range(1, parts):
        if hop > 1:
            total[...] = jnp.zeros_like(total)
        own = part_rows(lax.rem(vector + hop, parts), share)
        right_products(right, slots, 0, turn_of(right, slots, 0), own, 0, inter, env_right, total)
        send[hop - 1] = total[...].astype(jnp.bfloat16)


def both_kernel(slots, cut, listed, inter, env, send, keep, total, right, sem):
    lists = pltpu.make_async_copy(listed, right, sem)
    lists.start()
    total[...] = jnp.zeros_like(total)
    lists.wait()
    parts, share = send.shape[0] + 1, keep.shape[1]
    vector = lax.rem(lax.axis_index("term"), parts)
    begin, end = turn_of(right, slots, 0), turn_of(right, slots, 1)
    right_products(right, slots, begin, end, pl.ds(0, total.shape[1]), cut, inter, env, total)
    for hop in range(1, parts):
        rows = part_rows(lax.rem(vector + hop, parts), share)
        send[hop - 1] = total[:, rows, :].astype(jnp.bfloat16)
    keep[...] = total[:, part_rows(vector, share), :]


def own_kernel(slots, parts, listed, inter, env, keep, right, sem):
    lists = pltpu.make_async_copy(listed, right, sem)
    lists.start()
    keep[...] = jnp.zeros_like(keep)
    lists.wait()
    rows = part_rows(lax.rem(lax.axis_index("term"), parts), keep.shape[1])
    right_products(right, slots, 0, turn_of(right, slots, 0), rows, 0, inter, env, keep)


def finish_kernel(vectors, *refs):
    pieces, (out, held, sems) = refs[: 2 * vectors], refs[2 * vectors :]
    vector = lax.rem(lax.axis_index("term"), vectors)
    copies = []
    for hop in range(vectors):
        place = lax.rem(vector + vectors - hop, vectors)
        first = 0
        for part in range(2):
            source = pieces[2 * hop + part]
            span = pl.ds(first, source.shape[0])
            if hop > 0:
                held[hop - 1, span] = source[...].astype(jnp.float32)
                source = held.at[hop - 1, span]
            copies.append(
                pltpu.make_async_copy(source, out.at[span, place], sems.at[2 * hop + part])
            )
            copies[-1].start()
            first += span.size
    for copy in copies:
        copy.wait()


def shards(wave_tiles, left_env, right_env, send_list, left_tasks, right_tasks):
    sectors, terms = lax.axis_size("sector"), lax.axis_size("term")
    tiles, vectors, dim, _ = wave_tiles.shape
    term = lax.axis_index("term")
    blocks = terms // vectors
    rows, share = dim // blocks, dim // terms
    vector, block = term % vectors, term // vectors

    vmem = pl.BlockSpec(memory_space=pltpu.VMEM)
    hbm = pl.BlockSpec(memory_space=pl.ANY)
    send_slots = send_list.shape[1]
    tile_bytes = dim * dim * 2
    outgoing, env = pl.pallas_call(
        functools.partial(pack_kernel, vectors),
        out_shape=(
            jax.ShapeDtypeStruct((send_slots, dim, dim), jnp.bfloat16),
            jax.ShapeDtypeStruct((2, dim, dim), jnp.bfloat16),
        ),
        in_specs=[hbm, hbm, hbm, hbm],
        out_specs=(vmem, vmem),
        scratch_shapes=[
            pltpu.VMEM((tiles, dim, dim), jnp.bfloat16),
            pltpu.SMEM(send_list.shape, jnp.int32),
            pltpu.SemaphoreType.DMA((4,)),
        ],
        compiler_params=vmem_params(54 << 20),
        name="pack",
    )(send_list, wave_tiles, left_env, right_env)
    column = gather_far(env)
    received = lax.all_to_all(outgoing, "sector", split_axis=0, concat_axis=0, tiled=True)
    sides = gather_env(column)

    left_count, right_count = left_tasks.shape[2], right_tasks.shape[2]
    tasks = pl.pallas_call(
        tasks_kernel,
        out_shape=jax.ShapeDtypeStruct((8, max(left_count, right_count)), jnp.int32),
        in_specs=[vmem, vmem, hbm],
        out_specs=vmem,
        compiler_params=vmem_params(0),
        name="tasks",
    )(left_tasks[0, 0].T, right_tasks[0, 0].T, column[0])[None]
    bit = 1
    while bit < terms:
        tasks = jnp.concatenate([tasks, swap(tasks, "term", bit)], axis=0)
        bit *= 2

    def listed(first_row, count):
        rows = jnp.swapaxes(tasks[:, first_row : first_row + 3, :count], 0, 1).reshape(3, -1)
        group = (jnp.arange(terms * count, dtype=jnp.int32) // count) ^ term
        return rows[0], rows[1], rows[2], group

    left_env_tile, left_slot, left_inter, left_group = listed(0, left_count)
    right_inter, right_env_tile, right_sigma, right_group = listed(3, right_count)
    left_count, right_count = terms * left_count, terms * right_count
    left = jnp.concatenate(
        [
            env_place(left_group, left_env_tile),
            left_slot,
            left_group * INTER_TILES + left_inter,
        ]
    )
    turn = DEPTH * RIGHT_UNROLL
    slots = round_up(right_count + tiles * (DEPTH - 1), turn) + turn
    cut = tiles * 11 // 16
    inters = terms * INTER_TILES
    right = schedule(
        right_group * INTER_TILES + right_inter,
        env_place(right_group, right_env_tile),
        right_sigma,
        tiles,
        cut,
        DEPTH,
        turn,
        slots,
        inters,
    )
    block_bytes = rows * dim * 2
    env_tiles = terms * sectors
    env_bytes = env_tiles * tile_bytes
    near = env_bytes <= 2 << 20
    env_spec = vmem if near else hbm
    right_bytes = (tiles * 2 + inters) * block_bytes + env_bytes
    first_bytes = right_bytes + send_slots * tile_bytes + (2 * inters + env_tiles) * block_bytes
    right_params = vmem_params(right_bytes)

    def sent(count):
        return jax.ShapeDtypeStruct((vectors - 1, count, share, dim), jnp.bfloat16)

    def cost(part):
        flops = 2 * right_count * rows * dim * dim // part
        return pl.CostEstimate(flops=flops, bytes_accessed=12 << 20, transcendentals=0)

    inter, send_one, env_right = pl.pallas_call(
        functools.partial(first_kernel, left_count, slots, near),
        out_shape=(
            jax.ShapeDtypeStruct((inters + 1, rows, dim), jnp.bfloat16),
            sent(cut),
            jax.ShapeDtypeStruct((env_tiles, dim, dim), jnp.bfloat16),
        ),
        in_specs=[hbm, hbm, vmem] + [env_spec] * 4,
        out_specs=(vmem, vmem, vmem),
        scratch_shapes=[
            pltpu.VMEM((env_tiles, rows, dim), jnp.bfloat16),
            pltpu.VMEM((inters, rows, dim), jnp.float32),
            pltpu.VMEM((cut, share, dim), jnp.float32),
            pltpu.SMEM(left.shape, jnp.int32),
            pltpu.SMEM(right.shape, jnp.int32),
            pltpu.SemaphoreType.DMA((4,)),
        ],
        compiler_params=vmem_params(first_bytes + near * 2 * env_bytes),
        name="first_products",
    )(left, right, received, *sides[0], *sides[1])
    send_two, keep_two = pl.pallas_call(
        functools.partial(both_kernel, slots, cut),
        out_shape=(
            sent(tiles - cut),
            jax.ShapeDtypeStruct((tiles - cut, share, dim), jnp.float32),
        ),
        in_specs=[hbm, vmem, vmem],
        out_specs=(vmem, vmem),
        scratch_shapes=[
            pltpu.VMEM((tiles - cut, rows, dim), jnp.float32),
            pltpu.SMEM(right.shape, jnp.int32),
            pltpu.SemaphoreType.DMA,
        ],
        compiler_params=right_params,
        cost_estimate=cost(2),
        name="both_products",
    )(right, inter, env_right)
    keep_one = pl.pallas_call(
        functools.partial(own_kernel, slots, vectors),
        out_shape=jax.ShapeDtypeStruct((cut, share, dim), jnp.float32),
        in_specs=[hbm, vmem, vmem],
        out_specs=vmem,
        scratch_shapes=[pltpu.SMEM(right.shape, jnp.int32), pltpu.SemaphoreType.DMA],
        compiler_params=right_params,
        cost_estimate=cost(vectors),
        name="own_products",
    )(right, inter, env_right)
    pieces = [keep_one, keep_two]
    for hop in range(1, vectors):
        pairs = [
            (i, i // vectors * vectors + (i % vectors + hop) % vectors) for i in range(terms)
        ]
        pieces += [lax.ppermute(send[hop - 1], "term", pairs) for send in (send_one, send_two)]
    return pl.pallas_call(
        functools.partial(finish_kernel, vectors),
        out_shape=jax.ShapeDtypeStruct((tiles, vectors, share, dim), jnp.float32),
        in_specs=[vmem] * (2 * vectors),
        out_specs=hbm,
        scratch_shapes=[
            pltpu.VMEM((vectors - 1, tiles, share, dim), jnp.float32),
            pltpu.SemaphoreType.DMA((2 * vectors,)),
        ],
        compiler_params=vmem_params(3 * vectors * tiles * share * dim * 4),
        name="finish",
    )(*pieces)


def solution(mesh):
    in_specs = (
        P("sector", None, None, None),
        P("term", "sector", None, None),
        P("term", "sector", None, None),
        P("sector", None),
        P("term", "sector", None, None),
        P("term", "sector", None, None),
    )
    out_specs = P("sector", None, "term", None)
    return jax.shard_map(shards, mesh=mesh, in_specs=in_specs, out_specs=out_specs, check_vma=False)
```
